32 devices in a mesh: blk: 4 (over z), lat: 8 (over y, x, core).
Axes of the slice: x: 2, y: 2, z: 4, core: 2. Of those that a mesh axis runs over, the one named last changes fastest.
Arguments:
- ice_area: float32 [5, 12, 256, 4096], P(None, None, 'lat', 'blk'), may hold values from 0.05 to 1
- departure_weights: int32 [9, 256, 4096], P(None, 'lat', 'blk'), may hold values from 0 to 4096, as said below
- weld_rate: float32 [256, 4096], P('lat', 'blk'), may hold values from 0.1 to 1
- ice_cover: int32 [256, 4], P('lat', 'blk'), may hold values from 0 to 1, as said below
- wave_ocean: float32 [32, 25, 32, 1024], P(('blk', 'lat')), may hold values from 0.02 to 0.5
- ocean_route: int32 [32, 32], P(('blk', 'lat')), may hold values from 0 to 31, each once within a row
Outputs:
- new_area: float32 [5, 12, 256, 4096], P(None, None, 'lat', 'blk')
The draws below stay inside these ranges and needn't reach their ends.
Inputs may be any that keep to these rules, and one draw needn't show every extreme that they name: `departure_weights`: the nine weights of a cell sum to 4096; each off-centre weight is below 410. `ice_cover`: each device's count of ice-covered rows is a multiple of 4, from 4 to 32; in every longitude band the 8 devices' counts are 4, 8, ..., 32 in some order, so a band holds exactly 144 ice-covered blocks. `ocean_route`: each row is a permutation: every ocean device sends one wave block to every ice device.
All inputs are finite; a program needn't handle non-finite values.
Results may differ from the reference program's by a relative error of at most 0.0001.
Values sent between devices are 32-bit elements; how exact they have to be, the bound alone decides.
No kernel may reach another device: no remote copies, remote signals or barrier semaphores. Data moves between devices by JAX's collectives and lax.ppermute only.
A program may use at most 192 MiB of HBM per device.

```python
import math
import jax
import jax.numpy as jnp
import numpy as np
from jax import lax

NCAT = 5
NFSD = 12
FREQ = 25
TY = 32
TX = 1024
BANDS = 8
LON_BANDS = 4
NY = 256
NX = 4096
MINI = 1024
SLOTS = 4
N_BLK = 4
N_LAT = 8
DEVICES = 32


def draw_departure_weights(key, part):
    side_weights = jax.random.randint(key, (8, NY, NX), 0, 410, dtype=jnp.int32)
    side_weights = side_weights.at[:, 0, 0].set(0)
    centre = 4096 - jnp.sum(side_weights, axis=0, keepdims=True)
    return jnp.concatenate([side_weights[:4], centre, side_weights[4:]], axis=0).astype(jnp.int32)


def draw_ice_cover(key, part):
    order_key, rank_key = jax.random.split(jax.random.fold_in(key, 7))
    ramp = SLOTS * (jnp.arange(BANDS, dtype=jnp.int32) + 1)
    orders = jax.vmap(lambda sub_key: jax.random.permutation(sub_key, BANDS))(jax.random.split(order_key, LON_BANDS))
    counts = ramp[orders]
    ranks = jax.vmap(lambda sub_key: jax.random.permutation(sub_key, TY))(jax.random.split(rank_key, LON_BANDS * BANDS))
    ranks = ranks.reshape(LON_BANDS, BANDS, TY)
    covered = (ranks < counts[:, :, None]).astype(jnp.int32)
    return jnp.transpose(covered, (1, 2, 0)).reshape(NY, LON_BANDS).astype(jnp.int32)


def block_levels(key, shape, cuts, smallest, top_value):
    loudness = 1.0
    for dim, parts in cuts:
        heights = jax.random.uniform(jax.random.fold_in(jax.random.fold_in(key, 6), dim), (parts,), jnp.float32, smallest / len(cuts), top_value / len(cuts))
        loudness = loudness * jnp.repeat(jnp.exp(heights), shape[dim] // parts).reshape((-1,) + (1,) * (len(shape) - 1 - dim))
    return loudness


def setup_inputs(seed: int = 0) -> dict:
    key_of = jax.random.split(jax.random.key(seed), 7)
    ice_area = jnp.clip(0.05 + 0.95 * jax.random.uniform(key_of[0], (NCAT, NFSD, NY, NX), jnp.float32) ** block_levels(key_of[0], (NCAT, NFSD, NY, NX), ((2, 8), (3, 4)), -0.2, 0.2), 0.05, 1.0)
    departure_weights = draw_departure_weights(jax.random.fold_in(key_of[6], 71), 0)
    weld_rate = jnp.clip(jnp.exp(math.log(1.0) - 2.3025851 * jax.random.uniform(key_of[2], (NY, NX), jnp.float32) ** block_levels(key_of[2], (NY, NX), ((0, 8), (1, 4)), -0.2, 0.2)), 0.1, 1.0)
    ice_cover = draw_ice_cover(jax.random.fold_in(key_of[6], 71), 0)
    wave_ocean = jnp.clip(jnp.exp(math.log(0.5) - 3.218876 * jax.random.uniform(key_of[4], (DEVICES, FREQ, DEVICES, MINI), jnp.float32) ** block_levels(key_of[4], (DEVICES, FREQ, DEVICES, MINI), ((0, 32),), -0.2, 0.2)), 0.02, 0.5)
    ocean_route = jax.vmap(lambda own: jax.random.permutation(own, DEVICES))(jax.random.split(key_of[5], DEVICES)).reshape((DEVICES, DEVICES)).astype(jnp.int32)
    return dict(ice_area=ice_area, departure_weights=departure_weights, weld_rate=weld_rate, ice_cover=ice_cover, wave_ocean=wave_ocean, ocean_route=ocean_route)


fracture_step = 0.1


def fsd_tables():
    floe_index = np.arange(NFSD)
    kernel = 0.06 / (1.0 + np.abs(floe_index[:, None] - floe_index[None, :]))
    lower = np.where(floe_index[None, :] < floe_index[:, None], kernel, 0.0)
    diag_table = np.zeros((NFSD, NFSD))
    for index in range(NFSD - 1):
        diag_table[index + 1, index] = 0.06
    diag_table[NFSD - 1, NFSD - 1] = 0.06
    respond = (floe_index[None, :] / (NFSD - 1.0)) * (np.arange(FREQ)[:, None] + 1.0) / FREQ
    thickness = 1.0 / (1.0 + 0.5 * np.arange(NCAT))
    spread = np.where(floe_index[:, None] < floe_index[None, :], 1.0 / np.maximum(floe_index[None, :], 1), 0.0)
    return (jnp.asarray(kernel, jnp.float32), jnp.asarray(lower, jnp.float32), jnp.asarray(diag_table, jnp.float32), jnp.asarray(respond, jnp.float32), jnp.asarray(thickness, jnp.float32), jnp.asarray(spread, jnp.float32))


def rate_of(wave_field):
    respond = fsd_tables()[3]
    return jnp.einsum('fk,frx->krx', respond, wave_field, precision=lax.Precision.HIGHEST)


def column_physics(area_block, wave_rate, weld_field):
    highest = lax.Precision.HIGHEST
    kernel, lower, diag_table, respond, thickness, spread = fsd_tables()
    loss_rate = jnp.einsum('kj,njrx->nkrx', kernel, area_block, precision=highest)
    inner = jnp.einsum('kj,njrx->nkrx', lower, area_block, precision=highest)
    gain = 2.0 * area_block * inner + jnp.einsum('ki,nirx->nkrx', diag_table, area_block * area_block, precision=highest)
    welded = area_block + weld_field[None, None] * (gain - area_block * loss_rate)
    broken = fracture_step * thickness[:, None, None, None] * wave_rate[None] * welded
    return welded - broken + jnp.einsum('jk,nkrx->njrx', spread, broken, precision=highest)


def reference(ice_area, departure_weights, weld_rate, ice_cover, wave_ocean, ocean_route):
    order = jnp.argsort(ocean_route, axis=1).astype(jnp.int32)
    picked = jnp.take_along_axis(wave_ocean, order[:, None, :, None], axis=2)
    wave = jnp.transpose(picked, (1, 2, 0, 3)).reshape(FREQ, N_BLK, N_LAT, TY, TX)
    wave = jnp.transpose(wave, (0, 2, 3, 1, 4)).reshape(FREQ, NY, NX)
    wide = jnp.concatenate([ice_area[..., -1:], ice_area, ice_area[..., :1]], axis=3)
    ghost = wide[:, :, -1:, ::-1]
    bottom = jnp.zeros_like(wide[:, :, :1])
    padded = jnp.concatenate([bottom, wide, ghost], axis=2)
    weight_scale = departure_weights.astype(jnp.float32) / 4096.0
    moved = jnp.zeros(ice_area.shape, jnp.float32)
    for shift_y in range(3):
        for shift_x in range(3):
            moved = moved + weight_scale[3 * shift_y + shift_x] * padded[:, :, shift_y:shift_y + NY, shift_x:shift_x + NX]
    covered = jnp.repeat(ice_cover, TX, axis=1) > 0

    def band_step(block_index, result):
        first_row = (block_index * TY).astype(jnp.int32)
        piece = lax.dynamic_slice_in_dim(moved, first_row, TY, 2)
        wave_piece = lax.dynamic_slice_in_dim(wave, first_row, TY, 1)
        weld_piece = lax.dynamic_slice_in_dim(weld_rate, first_row, TY, 0)
        mask_piece = lax.dynamic_slice_in_dim(covered, first_row, TY, 0)
        worked = column_physics(piece, rate_of(wave_piece), weld_piece)
        return lax.dynamic_update_slice_in_dim(result, jnp.where(mask_piece[None, None], worked, piece), first_row, 2)

    return lax.fori_loop(0, NY // TY, band_step, moved)
```

```python
import functools

import jax
import jax.numpy as jnp
import ml_dtypes
import numpy as np
from jax import lax
from jax.experimental import pallas as pl
from jax.experimental.pallas import tpu as pltpu
from jax.sharding import PartitionSpec as P

NCAT = 5
NFSD = 12
FREQ = 25
PLANES = NCAT * NFSD
LANES = 128
SUB = 8
PITCH = 24
EXT = 48
AXES = ("blk", "lat")

fracture_step = 0.1
weld_scale = 840.0 / 1024.0


def weld_table():
    index = np.arange(NFSD)
    apart = index[:, None] - index[None, :]
    exact = np.where(apart > 0, 1.0, -1.0) / (1.0 + np.abs(apart)) * weld_scale
    high = exact.astype(ml_dtypes.bfloat16).astype(np.float64)
    low = exact - high
    kept = [0, 1, 2, 3, 8, 9, 10, 11]
    assert not np.delete(low, kept, axis=1).any()
    joined = np.concatenate([high, high, low[:, kept]], axis=1)
    return np.kron(joined, np.eye(SUB)).astype(ml_dtypes.bfloat16)


def pack_kernel(
    blk_count, lat_count, wave, ice, route, message, rows_a, rows_b,
    wave_buf, west_buf, east_buf, sums, columns, wave_sem, col_sem, row_sem,
):
    freq_count, dests, cells = wave.shape
    parts = wave_sem.shape[0]
    step = freq_count // parts
    tile_cols = ice.shape[2]
    tile_rows = ice.shape[1]
    chunks = tile_cols // LANES
    me_b = lax.axis_index("blk")
    me_l = lax.axis_index("lat")

    col_copies = [
        pltpu.make_async_copy(ice.at[:, :, pl.ds(0, LANES)], west_buf, col_sem.at[0]),
        pltpu.make_async_copy(
            ice.at[:, :, pl.ds(tile_cols - LANES, LANES)], east_buf, col_sem.at[1]
        ),
    ]
    wave_copies = [
        pltpu.make_async_copy(
            wave.at[pl.ds(p * step, step)], wave_buf.at[pl.ds(p * step, step)], wave_sem.at[p]
        )
        for p in range(parts)
    ]
    odd = lax.rem(me_l, 2) == 1
    first = jnp.where(odd, 0, tile_rows - 1)
    second = jnp.where(odd, tile_rows - 1, 0)
    row_copies = []
    for j in range(chunks):
        for which, (row, out) in enumerate(((first, rows_a), (second, rows_b))):
            row_copies.append(
                pltpu.make_async_copy(
                    ice.at[:, row, pl.ds(j * LANES, LANES)],
                    out.at[j, pl.ds(0, PLANES), :],
                    row_sem.at[which, j],
                )
            )
    for copy in col_copies + wave_copies + row_copies:
        copy.start()

    lane = lax.broadcasted_iota(jnp.int32, (SUB, LANES), 1)
    for side, (buf, from_lane) in enumerate(((west_buf, 0), (east_buf, LANES - 1))):
        col_copies[side].wait()

        def gather(p, parts_of):
            shift = lax.rem(p - from_lane + LANES, LANES)
            return tuple(
                jnp.where(lane == p, pltpu.roll(buf[p, SUB * i : SUB * i + SUB, :], shift, 1), part)
                for i, part in enumerate(parts_of)
            )

        got = tuple(jnp.zeros((SUB, LANES), jnp.float32) for _ in range(tile_rows // SUB))
        got = lax.fori_loop(0, PLANES, gather, got, unroll=4)
        half = len(got) // 2
        for i in range(half):
            columns[side, SUB * i : SUB * i + SUB, :] = jnp.where(
                lane < 64, got[i], pltpu.roll(got[i + half], 64, 1)
            )

    def send_columns(d, _):
        to_b = d // lat_count
        last_col = (to_b == lax.rem(me_b + 1, blk_count)) | (
            to_b == lax.rem(2 * blk_count - 2 - me_b, blk_count)
        )
        side = jnp.where(last_col, 1, 0)
        for i in range(2):
            message[d, SUB + SUB * i : 2 * SUB + SUB * i, :] = columns[side, SUB * i : SUB * i + SUB, :]
        return 0

    lax.fori_loop(0, dests, send_columns, 0, unroll=4)

    for copy in wave_copies:
        copy.wait()
    pieces = cells // LANES
    for group in range(dests // SUB):
        for j in range(pieces):
            total = jnp.zeros((SUB, LANES), jnp.float32)
            for f in range(freq_count):
                total = total + wave_buf[
                    f, SUB * group : SUB * group + SUB, LANES * j : LANES * j + LANES
                ] * np.float32((f + 1.0) / freq_count)
            sums[pl.ds(SUB * SUB * group + j, SUB, stride=SUB), :] = total

    def send_sums(m, _):
        message[route[0, m], 0:SUB, :] = sums[pl.ds(pl.multiple_of(m * SUB, SUB), SUB), :]
        return 0

    lax.fori_loop(0, dests, send_sums, 0, unroll=4)
    for copy in row_copies:
        copy.wait()


def pack(ice, wave, route, blk_count, lat_count):
    planes, tile_rows, tile_cols = ice.shape
    freq_count, dests, cells = wave.shape
    chunks = tile_cols // LANES
    return pl.pallas_call(
        functools.partial(pack_kernel, blk_count, lat_count),
        out_shape=(
            jax.ShapeDtypeStruct((dests, PITCH, LANES), jnp.float32),
            jax.ShapeDtypeStruct((chunks, 64, LANES), jnp.float32),
            jax.ShapeDtypeStruct((chunks, 64, LANES), jnp.float32),
        ),
        in_specs=[
            pl.BlockSpec(memory_space=pl.ANY),
            pl.BlockSpec(memory_space=pl.ANY),
            pl.BlockSpec(memory_space=pltpu.SMEM),
        ],
        out_specs=(
            pl.BlockSpec(memory_space=pltpu.VMEM),
            pl.BlockSpec(memory_space=pl.ANY),
            pl.BlockSpec(memory_space=pl.ANY),
        ),
        scratch_shapes=[
            pltpu.VMEM((freq_count, dests, cells), jnp.float32),
            pltpu.VMEM((planes, tile_rows, LANES), jnp.float32),
            pltpu.VMEM((planes, tile_rows, LANES), jnp.float32),
            pltpu.VMEM((dests * SUB, LANES), jnp.float32),
            pltpu.VMEM((2, 16, LANES), jnp.float32),
            pltpu.SemaphoreType.DMA((5,)),
            pltpu.SemaphoreType.DMA((2,)),
            pltpu.SemaphoreType.DMA((2, chunks)),
        ],
        compiler_params=pltpu.CompilerParams(vmem_limit_bytes=24 * 1024 * 1024),
        name="pack",
    )(wave, ice, route)


def step_kernel(
    blk_count, lat_count, cells,
    cover, ice, weights, weld, received, rows_a, rows_b, table, out,
    ext, scaled, weld_now, rate, ghosts, cols, moved,
):
    n = pl.program_id(0)
    tile_rows, tile_cols = weld.shape
    bands = tile_rows // SUB
    chunks = tile_cols // LANES
    plane_pitch = chunks * EXT
    lane = lax.broadcasted_iota(jnp.int32, (SUB, LANES), 1)
    sublane = lax.broadcasted_iota(jnp.int32, (SUB, LANES), 0)
    me_b = lax.axis_index("blk")
    me_l = lax.axis_index("lat")

    def shifted(pieces, west, east):
        to_right = [pltpu.roll(piece, 1, 1) for piece in pieces]
        to_left = [pltpu.roll(piece, LANES - 1, 1) for piece in pieces]
        from_west = [
            jnp.where(lane == 0, to_right[j - 1] if j else west, to_right[j])
            for j in range(chunks)
        ]
        from_east = [
            jnp.where(lane == LANES - 1, to_left[j + 1] if j + 1 < chunks else east, to_left[j])
            for j in range(chunks)
        ]
        return from_west, pieces, from_east

    @pl.when(n == 0)
    def prepare():
        top = me_l == lat_count - 1
        bottom = me_l == 0
        odd = lax.rem(me_l, 2) == 1
        west_b = lax.rem(me_b + blk_count - 1, blk_count)
        east_b = lax.rem(me_b + 1, blk_count)
        above_l = jnp.minimum(me_l + 1, lat_count - 1)
        below_l = jnp.maximum(me_l - 1, 0)

        def block(b, l):
            return pl.multiple_of((b * lat_count + l) * PITCH + SUB, SUB)

        for side, b in enumerate((west_b, east_b)):
            start = block(b, me_l)
            for i in range(2):
                packed = received[pl.ds(start + SUB * i, SUB), :]
                cols[side, SUB * i : SUB * i + SUB, :] = packed
                cols[side, 16 + SUB * i : 16 + SUB * i + SUB, :] = pltpu.roll(packed, 64, 1)

        def corner(b, l, last_row):
            start = block(b, l)
            low = received[pl.ds(start, SUB), :][0:1, :]
            high = pltpu.roll(received[pl.ds(start + SUB, SUB), :], 64, 1)[7:8, :]
            line = jnp.where(last_row, high, low)
            spread = jnp.broadcast_to(line, (SUB, LANES))
            return [
                jnp.sum(jnp.where(lane == SUB * q + sublane, spread, 0.0), axis=1, keepdims=True)
                for q in range(SUB)
            ]

        below_corners = [corner(b, below_l, True) for b in (west_b, east_b)]
        above_corners = [
            corner(jnp.where(top, fold_b, b), above_l, top)
            for fold_b, b in (
                (lax.rem(blk_count - me_b, blk_count), west_b),
                (lax.rem(2 * blk_count - 2 - me_b, blk_count), east_b),
            )
        ]
        backwards = LANES - 1 - lane
        for q in range(SUB):
            band = pl.ds(SUB * q, SUB)
            below = [
                jnp.where(bottom, 0.0, jnp.where(odd, rows_a[j, band, :], rows_b[j, band, :]))
                for j in range(chunks)
            ]
            above = [
                jnp.where(odd, rows_b[j, band, :], rows_a[j, band, :]) for j in range(chunks)
            ]
            folded = [
                jnp.take_along_axis(above[chunks - 1 - j], backwards, axis=1)
                for j in range(chunks)
            ]
            above = [jnp.where(top, folded[j], above[j]) for j in range(chunks)]
            for side, (pieces, corners) in enumerate(
                ((below, below_corners), (above, above_corners))
            ):
                ends = [jnp.broadcast_to(corners[s][q], (SUB, LANES)) for s in range(2)]
                if side == 0:
                    ends = [jnp.where(bottom, 0.0, end) for end in ends]
                for dx, line in enumerate(shifted(pieces, *ends)):
                    for j in range(chunks):
                        ghosts[side, dx, j, band, :] = line[j]

        per_row = tile_cols // cells
        for i in range(bands):
            mask = jnp.zeros((SUB, LANES), jnp.float32)
            for r in range(SUB):
                here = (cover[0, SUB * i + r] > 0).astype(jnp.float32)
                mask = jnp.where(sublane == r, here, mask)
            for j in range(chunks):
                own = (slice(SUB * i, SUB * i + SUB), slice(LANES * j, LANES * j + LANES))
                first = (per_row * SUB * i + j * LANES // cells) * PITCH + j % (cells // LANES)
                got = received[pl.ds(first, SUB, stride=per_row * PITCH), :]
                rate[own] = got * mask
                weld_now[own] = weld[own] * mask * np.float32(0.06 / weld_scale)
                for w in range(9):
                    scaled[(w,) + own] = weights[(w,) + own].astype(jnp.float32) * np.float32(
                        1.0 / 4096.0
                    )

    plane0 = n * NFSD
    for side in range(2):
        row = 7 if side == 0 else 8 + tile_rows
        for dx in range(3):
            for j in range(chunks):
                for k0 in (0, NFSD - SUB):
                    ext[dx, pl.ds(k0 * plane_pitch + j * EXT + row, SUB, stride=plane_pitch), :] = (
                        ghosts[side, dx, j, pl.ds(plane0 + k0, SUB), :]
                    )

    def widen(k, _):
        p = plane0 + k
        for i in range(bands):
            pieces = [
                ice[k, SUB * i : SUB * i + SUB, LANES * j : LANES * j + LANES]
                for j in range(chunks)
            ]
            west = pltpu.roll(cols[0, SUB * i : SUB * i + SUB, :], LANES - p, 1)
            east = pltpu.roll(cols[1, SUB * i : SUB * i + SUB, :], LANES - 1 - p, 1)
            for dx, line in enumerate(shifted(pieces, west, east)):
                for j in range(chunks):
                    start = pl.multiple_of(k * plane_pitch + j * EXT + SUB + SUB * i, SUB)
                    ext[dx, pl.ds(start, SUB), :] = line[j]
        return 0

    lax.fori_loop(0, NFSD, widen, 0)

    share = np.float32(fracture_step / 11.0) / (1.0 + 0.5 * n.astype(jnp.float32))

    def cells_of(i, jj, width):
        span = LANES * width
        rows = pl.ds(pl.multiple_of(i * SUB, SUB), SUB)
        for s in range(width):
            j = jj * width + s
            columns = pl.ds(pl.multiple_of(j * LANES, LANES), LANES)
            factors = [scaled[w, rows, columns] for w in range(9)]
            for k in range(NFSD):
                total = None
                for w in range(9):
                    dy, dx = w // 3, w % 3
                    start = k * plane_pitch + j * EXT + i * SUB + 7 + dy
                    term = factors[w] * ext[dx, pl.ds(start, SUB), :]
                    total = term if total is None else total + term
                moved[SUB * k : SUB * k + SUB, LANES * s : LANES * s + LANES] = total
        whole = moved[...]
        high = whole.astype(jnp.bfloat16)
        low = (whole - high.astype(jnp.float32)).astype(jnp.bfloat16)
        stacked = jnp.concatenate([high, low, high[: 4 * SUB], high[8 * SUB :]], axis=0)
        exchange = jnp.dot(table[...], stacked, preferred_element_type=jnp.float32)
        columns = pl.ds(pl.multiple_of(jj * span, span), span)
        speed = weld_now[rows, columns]
        breaking = rate[rows, columns] * share
        carried = jnp.zeros((SUB, span), jnp.float32)
        welded = []
        own = [moved[SUB * k : SUB * k + SUB, :] for k in range(NFSD)]
        squares = [area * (area * np.float32(weld_scale)) for area in own]
        for k in range(NFSD):
            turn = own[k] * exchange[SUB * k : SUB * k + SUB, :]
            if k:
                turn = turn + squares[k - 1]
            if k == NFSD - 1:
                turn = turn + squares[k]
            welded.append(own[k] + speed * turn)
        for k in range(NFSD - 1, -1, -1):
            broken = breaking * welded[k]
            out[k, rows, columns] = welded[k] + (carried - np.float32(k) * broken)
            carried = carried + broken

    width = 2

    def tiles(t, _):
        cells_of(t // (chunks // width), lax.rem(t, chunks // width), width)
        return 0

    lax.fori_loop(0, bands * (chunks // width), tiles, 0)


def advance(cover, ice, weights, weld, received, rows_a, rows_b, blk_count, lat_count, cells):
    planes, tile_rows, tile_cols = ice.shape
    chunks = tile_cols // LANES
    table = jnp.asarray(weld_table())
    vmem = pl.BlockSpec(memory_space=pltpu.VMEM)
    block = pl.BlockSpec((NFSD, tile_rows, tile_cols), lambda n: (n, 0, 0))
    return pl.pallas_call(
        functools.partial(step_kernel, blk_count, lat_count, cells),
        grid=(planes // NFSD,),
        out_shape=jax.ShapeDtypeStruct(ice.shape, jnp.float32),
        in_specs=[pl.BlockSpec(memory_space=pltpu.SMEM), block] + [vmem] * 6,
        out_specs=block,
        scratch_shapes=[
            pltpu.VMEM((3, NFSD * chunks * EXT, LANES), jnp.float32),
            pltpu.VMEM((9, tile_rows, tile_cols), jnp.float32),
            pltpu.VMEM((tile_rows, tile_cols), jnp.float32),
            pltpu.VMEM((tile_rows, tile_cols), jnp.float32),
            pltpu.VMEM((2, 3, chunks, 64, LANES), jnp.float32),
            pltpu.VMEM((2, tile_rows, LANES), jnp.float32),
            pltpu.VMEM((NFSD * SUB, 2 * LANES), jnp.float32),
        ],
        compiler_params=pltpu.CompilerParams(vmem_limit_bytes=40 * 1024 * 1024),
        name="advance",
    )(cover, ice, weights, weld, received, rows_a, rows_b, table)


def on_device(ice_area, departure_weights, weld_rate, ice_cover, wave_ocean, ocean_route):
    cat_count, floe_count, tile_rows, tile_cols = ice_area.shape
    lat_count = lax.axis_size("lat")
    blk_count = lax.axis_size("blk")
    cells = wave_ocean.shape[3]
    dests = wave_ocean.shape[2]
    ice = ice_area.reshape(cat_count * floe_count, tile_rows, tile_cols)
    message, rows_a, rows_b = pack(ice, wave_ocean[0], ocean_route, blk_count, lat_count)
    received = lax.all_to_all(message, AXES, split_axis=0, concat_axis=0, tiled=True)

    pairs_a, pairs_b = [], []
    for b in range(blk_count):
        for l in range(lat_count):
            here = b * lat_count + l
            pairs_a.append((here, here ^ 1 if lat_count % 2 == 0 else here))
            if l == lat_count - 1:
                pairs_b.append((here, (blk_count - 1 - b) * lat_count + l))
            elif l > 0:
                pairs_b.append((here, here + 1 if l % 2 else here - 1))
    from_a = lax.ppermute(rows_a, AXES, pairs_a)
    from_b = lax.ppermute(rows_b, AXES, pairs_b)
    result = advance(
        ice_cover.reshape(1, tile_rows), ice, departure_weights, weld_rate,
        received.reshape(dests * PITCH, LANES), from_a, from_b, blk_count, lat_count, cells,
    )
    return result.reshape(ice_area.shape)


def solution(mesh):
    return jax.shard_map(
        on_device,
        mesh=mesh,
        in_specs=(
            P(None, None, "lat", "blk"),
            P(None, "lat", "blk"),
            P("lat", "blk"),
            P("lat", "blk"),
            P(("blk", "lat"), None, None, None),
            P(("blk", "lat"), None),
        ),
        out_specs=P(None, None, "lat", "blk"),
        check_vma=False,
    )
```

```python
import functools

import jax
import jax.numpy as jnp
import ml_dtypes
import numpy as np
from jax import lax
from jax.experimental import pallas as pl
from jax.experimental.pallas import tpu as pltpu
from jax.sharding import PartitionSpec as P

NCAT = 5
NFSD = 12
FREQ = 25
PLANES = NCAT * NFSD
LANES = 128
SUB = 8
EXT = 41
VMEM_LIMIT = 56 * 1024 * 1024
AXES = ("blk", "lat")

fracture_step = 0.1
weld_scale = 840.0 / 1024.0


def weld_table():
    index = np.arange(NFSD)
    apart = index[:, None] - index[None, :]
    exact = np.where(apart > 0, 1.0, -1.0) / (1.0 + np.abs(apart)) * weld_scale
    high = exact.astype(ml_dtypes.bfloat16).astype(np.float64)
    low = exact - high
    kept = [0, 1, 2, 3, 8, 9, 10, 11]
    assert not np.delete(low, kept, axis=1).any()
    joined = np.concatenate([high, high, low[:, kept]], axis=1)
    return np.kron(joined, np.eye(SUB)).astype(ml_dtypes.bfloat16)


def pack_kernel(
    blk_count, lat_count, wave, ice, route, message, rows_a, rows_b, to_west, to_east,
    wave_buf, west_buf, east_buf, sums, corners, wave_sem, col_sem, row_sem,
):
    freq_count, dests, cells = wave.shape
    planes, tile_rows, tile_cols = ice.shape
    chunks = tile_cols // LANES
    bands = tile_rows // SUB
    me_b = lax.axis_index("blk")
    me_l = lax.axis_index("lat")

    col_copies, wave_copies = [], []
    for p in range(NCAT):
        own = pl.ds(p * NFSD, NFSD)
        for side, (buf, start) in enumerate(((west_buf, 0), (east_buf, tile_cols - LANES))):
            col_copies.append(
                pltpu.make_async_copy(
                    ice.at[own, :, pl.ds(start, LANES)], buf.at[own], col_sem.at[side, p]
                )
            )
    groups = wave_sem.shape[0]
    step = dests // groups
    for p in range(groups):
        own = pl.ds(p * step, step)
        wave_copies.append(
            pltpu.make_async_copy(wave.at[:, own, :], wave_buf.at[:, own, :], wave_sem.at[p])
        )
    odd = lax.rem(me_l, 2) == 1
    first = jnp.where(odd, 0, tile_rows - 1)
    second = jnp.where(odd, tile_rows - 1, 0)
    row_copies = []
    for j in range(chunks):
        for which, (row, out) in enumerate(((first, rows_a), (second, rows_b))):
            row_copies.append(
                pltpu.make_async_copy(
                    ice.at[:, row, pl.ds(j * LANES, LANES)],
                    out.at[j, pl.ds(0, planes), :],
                    row_sem.at[which, j],
                )
            )
    for copy in col_copies + wave_copies + row_copies:
        copy.start()

    lane = lax.broadcasted_iota(jnp.int32, (SUB, LANES), 1)
    columns = [jnp.zeros((SUB, LANES), jnp.float32) for _ in range(2 * bands)]
    for p in range(planes):
        if p % NFSD == 0:
            for copy in col_copies[2 * (p // NFSD) : 2 * (p // NFSD) + 2]:
                copy.wait()
        for i in range(bands):
            band = slice(SUB * i, SUB * i + SUB)
            ends = jnp.where(lane == 0, west_buf[p, band, :], east_buf[p, band, :])
            ends = pltpu.roll(ends, p, 1) if p else ends
            columns[i] = jnp.where(lane == p, ends, columns[i])
            columns[bands + i] = jnp.where(lane == (p - 1) % LANES, ends, columns[bands + i])
    east = [pltpu.roll(part, 1, 1) for part in columns[bands:]]
    for side, (parts_of, out) in enumerate(((columns[:bands], to_west), (east, to_east))):
        for i in range(bands // 2):
            out[SUB * i : SUB * i + SUB, :] = jnp.where(
                lane < 64, parts_of[i], pltpu.roll(parts_of[bands // 2 + i], 64, 1)
            )
        corners[2 * side : 2 * side + 1, :] = parts_of[0][0:1, :]
        corners[2 * side + 1 : 2 * side + 2, :] = parts_of[bands - 1][SUB - 1 : SUB, :]

    for group in range(dests // SUB):
        band = slice(SUB * group, SUB * group + SUB)
        if group * SUB % step == 0:
            wave_copies[group * SUB // step].wait()
        for j in range(cells // LANES):
            chunk = slice(LANES * j, LANES * j + LANES)
            total = wave_buf[0, band, chunk] * np.float32(1.0 / freq_count)
            for f in range(1, freq_count):
                total = total + wave_buf[f, band, chunk] * np.float32((f + 1.0) / freq_count)
            sums[j, band, :] = total

    side_of = []
    for to_b in range(blk_count):
        last_col = (to_b == lax.rem(me_b + 1, blk_count)) | (
            to_b == lax.rem(2 * blk_count - 2 - me_b, blk_count)
        )
        side_of.append(jnp.where(last_col, 2, 0))
    row_of = [jnp.where(to_l < me_l, 0, 1) for to_l in range(lat_count)]
    for m in range(dests):
        to = route[0, m]
        for j in range(cells // LANES):
            message[to, :, LANES * j : LANES * j + LANES] = sums[j, m : m + 1, :]
        which = side_of[m // lat_count] + row_of[m % lat_count]
        message[m, :, cells : cells + LANES] = corners[pl.ds(which, 1), :]
    for copy in row_copies:
        copy.wait()


def pack(ice, wave, route, blk_count, lat_count):
    planes, tile_rows, tile_cols = ice.shape
    freq_count, dests, cells = wave.shape
    chunks = tile_cols // LANES
    hbm = pl.BlockSpec(memory_space=pl.ANY)
    vmem = pl.BlockSpec(memory_space=pltpu.VMEM)
    rows = jax.ShapeDtypeStruct((chunks, 64, LANES), jnp.float32)
    column = jax.ShapeDtypeStruct((tile_rows // 2, LANES), jnp.float32)
    return pl.pallas_call(
        functools.partial(pack_kernel, blk_count, lat_count),
        out_shape=(
            jax.ShapeDtypeStruct((dests, 1, cells + LANES), jnp.float32),
            rows, rows, column, column,
        ),
        in_specs=[hbm, hbm, pl.BlockSpec(memory_space=pltpu.SMEM)],
        out_specs=(vmem,) * 5,
        scratch_shapes=[
            pltpu.VMEM((freq_count, dests, cells), jnp.float32),
            pltpu.VMEM((planes, tile_rows, LANES), jnp.float32),
            pltpu.VMEM((planes, tile_rows, LANES), jnp.float32),
            pltpu.VMEM((cells // LANES, dests, LANES), jnp.float32),
            pltpu.VMEM((SUB, LANES), jnp.float32),
            pltpu.SemaphoreType.DMA((4,)),
            pltpu.SemaphoreType.DMA((2, NCAT)),
            pltpu.SemaphoreType.DMA((2, chunks)),
        ],
        compiler_params=pltpu.CompilerParams(vmem_limit_bytes=VMEM_LIMIT),
        name="pack",
    )(wave, ice, route)


def step_kernel(
    blk_count, lat_count, cells,
    cover, ice, weights, weld, received, rows_a, rows_b, west_col, east_col, table, out,
    ice_buf, out_buf, weight_buf, ext_even, ext_odd, scaled, weld_now, rate, ghosts, cols,
    moved_even, moved_odd, stacked_even, stacked_odd, exchange_table, ice_sem, weight_sem, out_sem,
):
    tile_rows, tile_cols = weld.shape
    bands = tile_rows // SUB
    chunks = tile_cols // LANES
    plane_pitch = chunks * EXT + 1
    lane = lax.broadcasted_iota(jnp.int32, (SUB, LANES), 1)
    sublane = lax.broadcasted_iota(jnp.int32, (SUB, LANES), 0)
    me_b = lax.axis_index("blk")
    me_l = lax.axis_index("lat")
    exts = (ext_even, ext_odd)
    moveds = (moved_even, moved_odd)
    stackeds = (stacked_even, stacked_odd)

    def category(n):
        return pl.ds(n * NFSD, NFSD)

    ice_copies = [
        pltpu.make_async_copy(ice.at[category(n)], ice_buf.at[category(n)], ice_sem.at[n])
        for n in range(NCAT)
    ]
    weight_copy = pltpu.make_async_copy(weights, weight_buf, weight_sem)
    out_copies = [
        pltpu.make_async_copy(out_buf.at[category(n)], out.at[category(n)], out_sem.at[n])
        for n in range(NCAT)
    ]
    ice_copies[0].start()
    weight_copy.start()
    for copy in ice_copies[1:]:
        copy.start()

    def shifted(pieces, west, east):
        to_right = [pltpu.roll(piece, 1, 1) for piece in pieces]
        to_left = [pltpu.roll(piece, LANES - 1, 1) for piece in pieces]
        from_west = [
            jnp.where(lane == 0, to_right[j - 1] if j else west, to_right[j])
            for j in range(chunks)
        ]
        from_east = [
            jnp.where(lane == LANES - 1, to_left[j + 1] if j + 1 < chunks else east, to_left[j])
            for j in range(chunks)
        ]
        return from_west, pieces, from_east

    top = me_l == lat_count - 1
    bottom = me_l == 0
    odd = lax.rem(me_l, 2) == 1
    west_b = lax.rem(me_b + blk_count - 1, blk_count)
    east_b = lax.rem(me_b + 1, blk_count)
    above_l = jnp.minimum(me_l + 1, lat_count - 1)
    below_l = jnp.maximum(me_l - 1, 0)

    half = tile_rows // 2
    for side, column in enumerate((west_col, east_col)):
        for i in range(bands // 2):
            packed = column[SUB * i : SUB * i + SUB, :]
            cols[side, SUB * i : SUB * i + SUB, :] = packed
            cols[side, half + SUB * i : half + SUB * i + SUB, :] = pltpu.roll(packed, 64, 1)

    def corner(b, l):
        line = received[b * lat_count + l, :, cells : cells + LANES]
        spread = jnp.broadcast_to(line, (SUB, LANES))
        return [
            jnp.sum(jnp.where(lane == SUB * q + sublane, spread, 0.0), axis=1, keepdims=True)
            for q in range(SUB)
        ]

    below_corners = [corner(b, below_l) for b in (west_b, east_b)]
    above_corners = [
        corner(jnp.where(top, fold_b, b), above_l)
        for fold_b, b in (
            (lax.rem(blk_count - me_b, blk_count), west_b),
            (lax.rem(2 * blk_count - 2 - me_b, blk_count), east_b),
        )
    ]
    backwards = LANES - 1 - lane
    for q in range(SUB):
        band = pl.ds(SUB * q, SUB)
        below = [
            jnp.where(bottom, 0.0, jnp.where(odd, rows_a[j, band, :], rows_b[j, band, :]))
            for j in range(chunks)
        ]
        above = [jnp.where(odd, rows_b[j, band, :], rows_a[j, band, :]) for j in range(chunks)]
        folded = [
            jnp.take_along_axis(above[chunks - 1 - j], backwards, axis=1) for j in range(chunks)
        ]
        above = [jnp.where(top, folded[j], above[j]) for j in range(chunks)]
        for side, (pieces, corners) in enumerate(((below, below_corners), (above, above_corners))):
            ends = [jnp.broadcast_to(corners[s][q], (SUB, LANES)) for s in range(2)]
            if side == 0:
                ends = [jnp.where(bottom, 0.0, end) for end in ends]
            for dx, line in enumerate(shifted(pieces, *ends)):
                for j in range(chunks):
                    ghosts[side, dx, j, band, :] = line[j]

    per_row = tile_cols // cells
    for r in range(tile_rows):
        for j in range(chunks):
            o = r * per_row + j * LANES // cells
            start = j * LANES % cells
            rate[r : r + 1, LANES * j : LANES * j + LANES] = received[o, :, start : start + LANES]
    for i in range(bands):
        mask = jnp.zeros((SUB, LANES), jnp.float32)
        for r in range(SUB):
            here = (cover[0, SUB * i + r] > 0).astype(jnp.float32)
            mask = jnp.where(sublane == r, here, mask)
        for j in range(chunks):
            own = (slice(SUB * i, SUB * i + SUB), slice(LANES * j, LANES * j + LANES))
            rate[own] = rate[own] * (mask * np.float32(fracture_step / 11.0))
            weld_now[own] = weld[own] * mask * np.float32(0.06 / weld_scale)

    def border(n):
        ext = exts[n % 2]
        for side in range(2):
            row = 7 if side == 0 else 8 + tile_rows
            for dx in range(3):
                for j in range(chunks):
                    for k0 in (0, NFSD - SUB):
                        start = k0 * plane_pitch + j * EXT + row
                        ext[dx, pl.ds(start, SUB, stride=plane_pitch), :] = ghosts[
                            side, dx, j, pl.ds(n * NFSD + k0, SUB), :
                        ]

    def widen(n, unit):
        ext = exts[n % 2]
        i = unit // NFSD
        k = unit - i * NFSD
        p = n * NFSD + k
        rows = pl.ds(pl.multiple_of(i * SUB, SUB), SUB)
        pieces = [ice_buf[p, rows, LANES * j : LANES * j + LANES] for j in range(chunks)]
        west = pltpu.roll(cols[0, rows, :], LANES - p, 1)
        east = pltpu.roll(cols[1, rows, :], LANES - 1 - p, 1)
        for dx, line in enumerate(shifted(pieces, west, east)):
            for j in range(chunks):
                ext[dx, pl.ds(k * plane_pitch + j * EXT + SUB + i * SUB, SUB), :] = line[j]

    width = 2
    span = LANES * width
    per_band = chunks // width
    tiles = bands * per_band

    def place(t):
        return t // per_band, lax.rem(t, per_band)

    def stencil(n, t, slot):
        ext, moved, stacked = exts[n % 2], moveds[slot], stackeds[slot]
        i, jj = place(t)
        rows = pl.ds(pl.multiple_of(i * SUB, SUB), SUB)
        for s in range(width):
            j = jj * width + s
            columns = pl.ds(pl.multiple_of(j * LANES, LANES), LANES)
            factors = [scaled[w, rows, columns] for w in range(9)]
            base = j * EXT + i * SUB + 7
            for k in range(NFSD):
                total = None
                for w in range(9):
                    dy, dx = w // 3, w % 3
                    term = factors[w] * ext[dx, pl.ds(base + k * plane_pitch + dy, SUB), :]
                    total = term if total is None else total + term
                moved[SUB * k : SUB * k + SUB, LANES * s : LANES * s + LANES] = total
        whole = moved[...]
        high = whole.astype(jnp.bfloat16)
        low = (whole - high.astype(jnp.float32)).astype(jnp.bfloat16)
        stacked[...] = jnp.concatenate([high, low, high[: 4 * SUB], high[8 * SUB :]], axis=0)

    def exchange_of(slot):
        return jnp.dot(exchange_table[...], stackeds[slot][...], preferred_element_type=jnp.float32)

    def finish(n, t, slot, exchange):
        moved = moveds[slot]
        i, jj = place(t)
        rows = pl.ds(pl.multiple_of(i * SUB, SUB), SUB)
        columns = pl.ds(pl.multiple_of(jj * span, span), span)
        speed = weld_now[rows, columns]
        breaking = rate[rows, columns] * np.float32(1.0 / (1.0 + 0.5 * n))
        own = [moved[SUB * k : SUB * k + SUB, :] for k in range(NFSD)]
        squares = [area * (area * np.float32(weld_scale)) for area in own]
        welded = []
        for k in range(NFSD):
            turn = own[k] * exchange[SUB * k : SUB * k + SUB, :]
            if k:
                turn = turn + squares[k - 1]
            if k == NFSD - 1:
                turn = turn + squares[k]
            welded.append(own[k] + speed * turn)
        carried = None
        for k in range(NFSD - 1, -1, -1):
            if k:
                broken = breaking * welded[k]
                change = broken * np.float32(-k)
                if carried is not None:
                    change = carried + change
                carried = broken if carried is None else carried + broken
            else:
                change = carried
            out_buf[n * NFSD + k, rows, columns] = welded[k] + change

    per_tile = bands * NFSD // tiles

    def pair(n, t, last):
        more = n + 1 < NCAT
        for s in range(2):
            exchange = exchange_of(s)
            if last and s == 1:
                if more:
                    for u in range(per_tile):
                        widen(n + 1, (t + s) * per_tile + u)
                    stencil(n + 1, 0, 0)
                finish(n, t + s, s, exchange)
            else:
                stencil(n, t + s + 1, 1 - s)
                finish(n, t + s, s, exchange)
                if more:
                    for u in range(per_tile):
                        widen(n + 1, (t + s) * per_tile + u)

    exchange_table[...] = table[...].astype(jnp.bfloat16)
    weight_copy.wait()
    for w in range(9):
        scaled[w] = weight_buf[w].astype(jnp.float32) * np.float32(1.0 / 4096.0)
    ice_copies[0].wait()
    border(0)

    def first_units(u, _):
        widen(0, u)
        return 0

    lax.fori_loop(0, bands * NFSD, first_units, 0, unroll=2)
    stencil(0, 0, 0)
    for n in range(NCAT):
        if n + 1 < NCAT:
            ice_copies[n + 1].wait()
            border(n + 1)

        def both(h, _):
            pair(n, h * 2, False)
            return 0

        lax.fori_loop(0, tiles // 2 - 1, both, 0)
        pair(n, tiles - 2, True)
        out_copies[n].start()
    for copy in out_copies:
        copy.wait()


def advance(
    cover, ice, weights, weld, received, rows_a, rows_b, west_col, east_col,
    blk_count, lat_count, cells,
):
    planes, tile_rows, tile_cols = ice.shape
    chunks = tile_cols // LANES
    table = jnp.asarray(weld_table().astype(np.float32))
    vmem = pl.BlockSpec(memory_space=pltpu.VMEM)
    hbm = pl.BlockSpec(memory_space=pl.ANY)
    tile = pltpu.VMEM((tile_rows, tile_cols), jnp.float32)
    ext = pltpu.VMEM((3, NFSD * (chunks * EXT + 1), LANES), jnp.float32)
    moved = pltpu.VMEM((NFSD * SUB, 2 * LANES), jnp.float32)
    stacked = pltpu.VMEM((2 * LANES, 2 * LANES), jnp.bfloat16)
    return pl.pallas_call(
        functools.partial(step_kernel, blk_count, lat_count, cells),
        out_shape=jax.ShapeDtypeStruct(ice.shape, jnp.float32),
        in_specs=[pl.BlockSpec(memory_space=pltpu.SMEM), hbm, hbm] + [vmem] * 7,
        out_specs=hbm,
        scratch_shapes=[
            pltpu.VMEM(ice.shape, jnp.float32),
            pltpu.VMEM(ice.shape, jnp.float32),
            pltpu.VMEM(weights.shape, jnp.int32),
            ext, ext,
            pltpu.VMEM(weights.shape, jnp.float32),
            tile, tile,
            pltpu.VMEM((2, 3, chunks, 64, LANES), jnp.float32),
            pltpu.VMEM((2, tile_rows, LANES), jnp.float32),
            moved, moved, stacked, stacked,
            pltpu.VMEM((NFSD * SUB, 2 * LANES), jnp.bfloat16),
            pltpu.SemaphoreType.DMA((NCAT,)),
            pltpu.SemaphoreType.DMA,
            pltpu.SemaphoreType.DMA((NCAT,)),
        ],
        compiler_params=pltpu.CompilerParams(vmem_limit_bytes=VMEM_LIMIT),
        name="advance",
    )(cover, ice, weights, weld, received, rows_a, rows_b, west_col, east_col, table)


def on_device(ice_area, departure_weights, weld_rate, ice_cover, wave_ocean, ocean_route):
    cat_count, floe_count, tile_rows, tile_cols = ice_area.shape
    lat_count = lax.axis_size("lat")
    blk_count = lax.axis_size("blk")
    assert lat_count % 2 == 0 and blk_count % 2 == 0 and blk_count > 2
    cells = wave_ocean.shape[3]
    ice = ice_area.reshape(cat_count * floe_count, tile_rows, tile_cols)
    message, rows_a, rows_b, to_west, to_east = pack(
        ice, wave_ocean[0], ocean_route, blk_count, lat_count
    )
    received = lax.all_to_all(message, AXES, split_axis=0, concat_axis=0, tiled=True)

    pairs_a, pairs_b = [], []
    for b in range(blk_count):
        for l in range(lat_count):
            here = b * lat_count + l
            pairs_a.append((here, here ^ 1))
            if l == lat_count - 1:
                pairs_b.append((here, (blk_count - 1 - b) * lat_count + l))
            elif l > 0:
                pairs_b.append((here, here + 1 if l % 2 else here - 1))
    from_a = lax.ppermute(rows_a, AXES, pairs_a)
    from_b = lax.ppermute(rows_b, AXES, pairs_b)
    ring = [(b, (b + 1) % blk_count) for b in range(blk_count)]
    west_col = lax.ppermute(to_east, "blk", ring)
    east_col = lax.ppermute(to_west, "blk", [(b, a) for a, b in ring])
    result = advance(
        ice_cover.reshape(1, tile_rows), ice, departure_weights, weld_rate,
        received, from_a, from_b, west_col, east_col, blk_count, lat_count, cells,
    )
    return result.reshape(ice_area.shape)


def solution(mesh):
    return jax.shard_map(
        on_device,
        mesh=mesh,
        in_specs=(
            P(None, None, "lat", "blk"),
            P(None, "lat", "blk"),
            P("lat", "blk"),
            P("lat", "blk"),
            P(("blk", "lat"), None, None, None),
            P(("blk", "lat"), None),
        ),
        out_specs=P(None, None, "lat", "blk"),
        check_vma=False,
    )
```

```python
import functools

import jax
import jax.numpy as jnp
import ml_dtypes
import numpy as np
from jax import lax
from jax.experimental import pallas as pl
from jax.experimental.pallas import tpu as pltpu
from jax.sharding import PartitionSpec as P

NCAT = 5
NFSD = 12
FREQ = 25
PLANES = NCAT * NFSD
LANES = 128
SUB = 8
EXT = 41
VMEM_LIMIT = 56 * 1024 * 1024
AXES = ("blk", "lat")

fracture_step = 0.1
weld_scale = 840.0 / 1024.0


def weld_table():
    index = np.arange(NFSD)
    apart = index[:, None] - index[None, :]
    exact = np.where(apart > 0, 1.0, -1.0) / (1.0 + np.abs(apart)) * weld_scale
    high = exact.astype(ml_dtypes.bfloat16).astype(np.float64)
    low = exact - high
    kept = [0, 1, 2, 3, 8, 9, 10, 11]
    assert not np.delete(low, kept, axis=1).any()
    joined = np.concatenate([high, high, low[:, kept]], axis=1)
    return np.kron(joined, np.eye(SUB)).astype(ml_dtypes.bfloat16)


def gather_edges(west_buf, east_buf, copies, planes, bands_of):
    lane = lax.broadcasted_iota(jnp.int32, (SUB, LANES), 1)
    west = [jnp.zeros((SUB, LANES), jnp.float32) for _ in bands_of]
    east = list(west)
    for p in range(planes):
        if p % NFSD == 0:
            for copy in copies[p // NFSD]:
                copy.wait()
        for i, start in enumerate(bands_of):
            band = slice(start, start + SUB)
            ends = jnp.where(lane == 0, west_buf[p, band, :], east_buf[p, band, :])
            ends = pltpu.roll(ends, p, 1) if p else ends
            west[i] = jnp.where(lane == p, ends, west[i])
            east[i] = jnp.where(lane == (p - 1) % LANES, ends, east[i])
    return west, [pltpu.roll(part, 1, 1) for part in east]


def wave_kernel(
    blk_count, lat_count, wave, ice, route_hbm, message, rows_a, rows_b,
    edge_rows, route, wave_buf, west_buf, east_buf, sums, corners, route_sem, wave_sem, col_sem, row_sem, send_sem,
):
    freq_count, dests, cells = wave.shape
    planes, tile_rows, tile_cols = ice.shape
    me_b = lax.axis_index("blk")
    me_l = lax.axis_index("lat")

    odd = lax.rem(me_l, 2) == 1
    first = jnp.where(odd, 0, tile_rows - 1)
    second = jnp.where(odd, tile_rows - 1, 0)
    chunks = tile_cols // LANES
    row_copies = []
    for j in range(chunks):
        for which, row in enumerate((first, second)):
            row_copies.append(
                pltpu.make_async_copy(
                    ice.at[:, row, pl.ds(j * LANES, LANES)],
                    edge_rows.at[which, j, pl.ds(0, planes), :],
                    row_sem.at[which, j],
                )
            )
    send_copies = [
        pltpu.make_async_copy(edge_rows.at[which], out, send_sem.at[which])
        for which, out in enumerate((rows_a, rows_b))
    ]
    for copy in row_copies:
        copy.start()
    col_copies = []
    for p in range(NCAT):
        own = pl.ds(p * NFSD, NFSD)
        col_copies.append(
            [
                pltpu.make_async_copy(
                    ice.at[own, pl.ds(row, SUB), pl.ds(start, LANES)],
                    buf.at[own, pl.ds(e * SUB, SUB), :],
                    col_sem.at[p, side, e],
                )
                for side, (buf, start) in enumerate(
                    ((west_buf, 0), (east_buf, tile_cols - LANES))
                )
                for e, row in enumerate((0, tile_rows - SUB))
            ]
        )
    groups = wave_sem.shape[0]
    step = dests // groups
    wave_copies = []
    for p in range(groups):
        own = pl.ds(p * step, step)
        wave_copies.append(
            pltpu.make_async_copy(wave.at[:, own, :], wave_buf.at[:, own, :], wave_sem.at[p])
        )
    route_copy = pltpu.make_async_copy(route_hbm, route, route_sem)
    route_copy.start()
    for copies in col_copies + [wave_copies]:
        for copy in copies:
            copy.start()

    ends = gather_edges(west_buf, east_buf, col_copies, planes, (0, SUB))
    for copy in row_copies:
        copy.wait()
    for copy in send_copies:
        copy.start()
    for side in range(2):
        corners[2 * side : 2 * side + 1, :] = ends[side][0][0:1, :]
        corners[2 * side + 1 : 2 * side + 2, :] = ends[side][1][SUB - 1 : SUB, :]

    for group in range(dests // SUB):
        band = slice(SUB * group, SUB * group + SUB)
        if group * SUB % step == 0:
            wave_copies[group * SUB // step].wait()
        for j in range(cells // LANES):
            chunk = slice(LANES * j, LANES * j + LANES)
            total = wave_buf[0, band, chunk] * np.float32(1.0 / freq_count)
            for f in range(1, freq_count):
                total = total + wave_buf[f, band, chunk] * np.float32((f + 1.0) / freq_count)
            sums[j, band, :] = total

    route_copy.wait()
    side_of = []
    for to_b in range(blk_count):
        last_col = (to_b == lax.rem(me_b + 1, blk_count)) | (
            to_b == lax.rem(2 * blk_count - 2 - me_b, blk_count)
        )
        side_of.append(jnp.where(last_col, 2, 0))
    row_of = [jnp.where(to_l < me_l, 0, 1) for to_l in range(lat_count)]
    for m in range(dests):
        to = route[0, m]
        for j in range(cells // LANES):
            message[to, :, LANES * j : LANES * j + LANES] = sums[j, m : m + 1, :]
        which = side_of[m // lat_count] + row_of[m % lat_count]
        message[m, :, cells : cells + LANES] = corners[pl.ds(which, 1), :]
    for copy in send_copies:
        copy.wait()


def pack_wave(ice, wave, route, blk_count, lat_count):
    planes, tile_rows, tile_cols = ice.shape
    freq_count, dests, cells = wave.shape
    chunks = tile_cols // LANES
    hbm = pl.BlockSpec(memory_space=pl.ANY)
    return pl.pallas_call(
        functools.partial(wave_kernel, blk_count, lat_count),
        out_shape=(
            jax.ShapeDtypeStruct((dests, 1, cells + LANES), jnp.float32),
            pltpu.HBM((chunks, 64, LANES), jnp.float32),
            pltpu.HBM((chunks, 64, LANES), jnp.float32),
        ),
        in_specs=[hbm] * 3,
        out_specs=(pl.BlockSpec(memory_space=pltpu.VMEM), hbm, hbm),
        scratch_shapes=[
            pltpu.VMEM((2, chunks, 64, LANES), jnp.float32),
            pltpu.SMEM(route.shape, jnp.int32),
            pltpu.VMEM((freq_count, dests, cells), jnp.float32),
            pltpu.VMEM((planes, 2 * SUB, LANES), jnp.float32),
            pltpu.VMEM((planes, 2 * SUB, LANES), jnp.float32),
            pltpu.VMEM((cells // LANES, dests, LANES), jnp.float32),
            pltpu.VMEM((SUB, LANES), jnp.float32),
            pltpu.SemaphoreType.DMA,
            pltpu.SemaphoreType.DMA((4,)),
            pltpu.SemaphoreType.DMA((NCAT, 2, 2)),
            pltpu.SemaphoreType.DMA((2, chunks)),
            pltpu.SemaphoreType.DMA((2,)),
        ],
        compiler_params=pltpu.CompilerParams(vmem_limit_bytes=VMEM_LIMIT),
        name="pack_wave",
    )(*[pltpu.with_memory_space_constraint(array, pltpu.HBM) for array in (wave, ice, route)])


def halo_kernel(ice, after, to_west, to_east, west_buf, east_buf, col_sem):
    planes, tile_rows, tile_cols = ice.shape
    bands = tile_rows // SUB
    col_copies = []
    for p in range(NCAT):
        own = pl.ds(p * NFSD, NFSD)
        col_copies.append(
            [
                pltpu.make_async_copy(
                    ice.at[own, :, pl.ds(start, LANES)], buf.at[own], col_sem.at[p, side]
                )
                for side, (buf, start) in enumerate(
                    ((west_buf, 0), (east_buf, tile_cols - LANES))
                )
            ]
        )
    for copies in col_copies:
        for copy in copies:
            copy.start()

    lane = lax.broadcasted_iota(jnp.int32, (SUB, LANES), 1)
    ends = gather_edges(
        west_buf, east_buf, col_copies, planes, tuple(range(0, tile_rows, SUB))
    )
    for parts_of, out in zip(ends, (to_west, to_east)):
        for i in range(bands // 2):
            out[SUB * i : SUB * i + SUB, :] = jnp.where(
                lane < 64, parts_of[i], pltpu.roll(parts_of[bands // 2 + i], 64, 1)
            )


def pack_halo(ice, after):
    planes, tile_rows, tile_cols = ice.shape
    hbm = pl.BlockSpec(memory_space=pl.ANY)
    vmem = pl.BlockSpec(memory_space=pltpu.VMEM)
    column = pltpu.VMEM((tile_rows // 2, LANES), jnp.float32)
    return pl.pallas_call(
        halo_kernel,
        out_shape=(column, column),
        in_specs=[hbm, hbm],
        out_specs=(vmem,) * 2,
        scratch_shapes=[
            pltpu.VMEM((planes, tile_rows, LANES), jnp.float32),
            pltpu.VMEM((planes, tile_rows, LANES), jnp.float32),
            pltpu.SemaphoreType.DMA((NCAT, 2)),
        ],
        compiler_params=pltpu.CompilerParams(vmem_limit_bytes=VMEM_LIMIT),
        name="pack_halo",
    )(*[pltpu.with_memory_space_constraint(array, pltpu.HBM) for array in (ice, after)])


def shifted(pieces, west, east):
    lane = lax.broadcasted_iota(jnp.int32, (SUB, LANES), 1)
    chunks = len(pieces)
    to_right = [pltpu.roll(piece, 1, 1) for piece in pieces]
    to_left = [pltpu.roll(piece, LANES - 1, 1) for piece in pieces]
    from_west = [to_right[0] if west is None else jnp.where(lane == 0, west, to_right[0])] + [
        jnp.where(lane == 0, to_right[j - 1], to_right[j]) for j in range(1, chunks)
    ]
    from_east = [
        jnp.where(lane == LANES - 1, to_left[j + 1], to_left[j]) for j in range(chunks - 1)
    ]
    from_east.append(
        to_left[-1] if east is None else jnp.where(lane == LANES - 1, east, to_left[-1])
    )
    return from_west, pieces, from_east


def step_kernel(
    blk_count, lat_count, cells,
    ice, weights, cover_hbm, weld_hbm, received_hbm, rows_a_hbm, rows_b_hbm, west_hbm, east_hbm,
    table_hbm, out,
    cover, weld, received, rows_a, rows_b, west_col, east_col, table,
    ice_buf, out_buf, weight_buf, ext_even, ext_odd, scaled, weld_now, rate, ghosts, cols,
    moved_even, moved_odd, stacked_even, stacked_odd, exchange_table,
    small_sem, ice_sem, weight_sem, out_sem,
):
    tile_rows, tile_cols = weld.shape
    bands = tile_rows // SUB
    chunks = tile_cols // LANES
    plane_pitch = chunks * EXT + 1
    lane = lax.broadcasted_iota(jnp.int32, (SUB, LANES), 1)
    sublane = lax.broadcasted_iota(jnp.int32, (SUB, LANES), 0)
    me_b = lax.axis_index("blk")
    me_l = lax.axis_index("lat")
    exts = (ext_even, ext_odd)
    moveds = (moved_even, moved_odd)
    stackeds = (stacked_even, stacked_odd)

    def category(n):
        return pl.ds(n * NFSD, NFSD)

    small_copies = [
        pltpu.make_async_copy(source, to, small_sem.at[c])
        for c, (source, to) in enumerate(
            (
                (rows_a_hbm, rows_a), (rows_b_hbm, rows_b), (west_hbm, west_col),
                (east_hbm, east_col), (received_hbm, received), (cover_hbm, cover),
                (weld_hbm, weld), (table_hbm, table),
            )
        )
    ]
    ice_copies = [
        pltpu.make_async_copy(ice.at[category(n)], ice_buf.at[category(n)], ice_sem.at[n])
        for n in range(NCAT)
    ]
    weight_copy = pltpu.make_async_copy(weights, weight_buf, weight_sem)
    out_copies = [
        pltpu.make_async_copy(out_buf.at[category(n)], out.at[category(n)], out_sem.at[n])
        for n in range(NCAT - 1)
    ]
    for copy in small_copies:
        copy.start()
    ice_copies[0].start()
    weight_copy.start()
    ice_copies[1].start()
    for copy in small_copies:
        copy.wait()

    top = me_l == lat_count - 1
    bottom = me_l == 0
    odd = lax.rem(me_l, 2) == 1
    west_b = lax.rem(me_b + blk_count - 1, blk_count)
    east_b = lax.rem(me_b + 1, blk_count)
    above_l = jnp.minimum(me_l + 1, lat_count - 1)
    below_l = jnp.maximum(me_l - 1, 0)

    half = tile_rows // 2
    for side, column in enumerate((west_col, east_col)):
        for i in range(bands // 2):
            packed = column[SUB * i : SUB * i + SUB, :]
            cols[side, SUB * i : SUB * i + SUB, :] = packed
            cols[side, half + SUB * i : half + SUB * i + SUB, :] = pltpu.roll(packed, 64, 1)

    def corner(b, l):
        line = received[b * lat_count + l, :, cells : cells + LANES]
        spread = jnp.broadcast_to(line, (SUB, LANES))
        return [
            jnp.sum(jnp.where(lane == SUB * q + sublane, spread, 0.0), axis=1, keepdims=True)
            for q in range(SUB)
        ]

    below_corners = [corner(b, below_l) for b in (west_b, east_b)]
    above_corners = [
        corner(jnp.where(top, fold_b, b), above_l)
        for fold_b, b in (
            (lax.rem(blk_count - me_b, blk_count), west_b),
            (lax.rem(2 * blk_count - 2 - me_b, blk_count), east_b),
        )
    ]
    backwards = LANES - 1 - lane
    for q in range(SUB):
        band = pl.ds(SUB * q, SUB)
        below = [
            jnp.where(bottom, 0.0, jnp.where(odd, rows_a[j, band, :], rows_b[j, band, :]))
            for j in range(chunks)
        ]
        above = [jnp.where(odd, rows_b[j, band, :], rows_a[j, band, :]) for j in range(chunks)]
        folded = [
            jnp.take_along_axis(above[chunks - 1 - j], backwards, axis=1) for j in range(chunks)
        ]
        above = [jnp.where(top, folded[j], above[j]) for j in range(chunks)]
        for side, (pieces, corners) in enumerate(((below, below_corners), (above, above_corners))):
            ends = [jnp.broadcast_to(corners[s][q], (SUB, LANES)) for s in range(2)]
            if side == 0:
                ends = [jnp.where(bottom, 0.0, end) for end in ends]
            for dx, line in enumerate(shifted(pieces, *ends)):
                for j in range(chunks):
                    ghosts[side, dx, j, band, :] = line[j]

    per_row = tile_cols // cells
    for r in range(tile_rows):
        for j in range(chunks):
            o = r * per_row + j * LANES // cells
            start = j * LANES % cells
            rate[r : r + 1, LANES * j : LANES * j + LANES] = received[o, :, start : start + LANES]
    for i in range(bands):
        mask = jnp.zeros((SUB, LANES), jnp.float32)
        for r in range(SUB):
            here = (cover[0, SUB * i + r] > 0).astype(jnp.float32)
            mask = jnp.where(sublane == r, here, mask)
        for j in range(chunks):
            own = (slice(SUB * i, SUB * i + SUB), slice(LANES * j, LANES * j + LANES))
            rate[own] = rate[own] * (mask * np.float32(fracture_step / 11.0))
            weld_now[own] = weld[own] * mask * np.float32(0.06 / weld_scale)

    def border(n):
        ext = exts[n % 2]
        for side in range(2):
            row = 7 if side == 0 else 8 + tile_rows
            for dx in range(3):
                for j in range(chunks):
                    for k0 in (0, NFSD - SUB):
                        start = k0 * plane_pitch + j * EXT + row
                        ext[dx, pl.ds(start, SUB, stride=plane_pitch), :] = ghosts[
                            side, dx, j, pl.ds(n * NFSD + k0, SUB), :
                        ]

    def widen(n, unit):
        ext = exts[n % 2]
        i = unit // NFSD
        k = unit - i * NFSD
        p = n * NFSD + k
        rows = pl.ds(pl.multiple_of(i * SUB, SUB), SUB)
        pieces = [ice_buf[p, rows, LANES * j : LANES * j + LANES] for j in range(chunks)]
        west = pltpu.roll(cols[0, rows, :], LANES - p, 1)
        east = pltpu.roll(cols[1, rows, :], LANES - 1 - p, 1)
        for dx, line in enumerate(shifted(pieces, west, east)):
            for j in range(chunks):
                ext[dx, pl.ds(k * plane_pitch + j * EXT + SUB + i * SUB, SUB), :] = line[j]

    width = 2
    span = LANES * width
    per_band = chunks // width
    tiles = bands * per_band

    def place(t):
        return t // per_band, lax.rem(t, per_band)

    def stencil(n, t, slot):
        ext, moved, stacked = exts[n % 2], moveds[slot], stackeds[slot]
        i, jj = place(t)
        rows = pl.ds(pl.multiple_of(i * SUB, SUB), SUB)
        for s in range(width):
            j = jj * width + s
            columns = pl.ds(pl.multiple_of(j * LANES, LANES), LANES)
            factors = [scaled[w, rows, columns] for w in range(9)]
            base = j * EXT + i * SUB + 7
            for k in range(NFSD):
                total = None
                for w in range(9):
                    dy, dx = w // 3, w % 3
                    term = factors[w] * ext[dx, pl.ds(base + k * plane_pitch + dy, SUB), :]
                    total = term if total is None else total + term
                moved[SUB * k : SUB * k + SUB, LANES * s : LANES * s + LANES] = total
        whole = moved[...]
        high = whole.astype(jnp.bfloat16)
        low = (whole - high.astype(jnp.float32)).astype(jnp.bfloat16)
        stacked[...] = jnp.concatenate([high, low, high[: 4 * SUB], high[8 * SUB :]], axis=0)

    def exchange_of(slot):
        return jnp.dot(exchange_table[...], stackeds[slot][...], preferred_element_type=jnp.float32)

    def finish(n, t, slot, exchange):
        moved = moveds[slot]
        i, jj = place(t)
        rows = pl.ds(pl.multiple_of(i * SUB, SUB), SUB)
        columns = pl.ds(pl.multiple_of(jj * span, span), span)
        speed = weld_now[rows, columns]
        breaking = rate[rows, columns] * np.float32(1.0 / (1.0 + 0.5 * n))
        own = [moved[SUB * k : SUB * k + SUB, :] for k in range(NFSD)]
        squares = [area * (area * np.float32(weld_scale)) for area in own]
        welded = []
        for k in range(NFSD):
            turn = own[k] * exchange[SUB * k : SUB * k + SUB, :]
            if k:
                turn = turn + squares[k - 1]
            if k == NFSD - 1:
                turn = turn + squares[k]
            welded.append(own[k] + speed * turn)
        carried = None
        for k in range(NFSD - 1, -1, -1):
            if k:
                broken = breaking * welded[k]
                change = broken * np.float32(-k)
                if carried is not None:
                    change = carried + change
                carried = broken if carried is None else carried + broken
            else:
                change = carried
            out_buf[n * NFSD + k, rows, columns] = welded[k] + change

    per_tile = bands * NFSD // tiles

    def pair(n, t, last):
        more = n + 1 < NCAT
        for s in range(2):
            exchange = exchange_of(s)
            if last and s == 1:
                if more:
                    for u in range(per_tile):
                        widen(n + 1, (t + s) * per_tile + u)
                    stencil(n + 1, 0, 0)
                finish(n, t + s, s, exchange)
            else:
                stencil(n, t + s + 1, 1 - s)
                finish(n, t + s, s, exchange)
                if more:
                    for u in range(per_tile):
                        widen(n + 1, (t + s) * per_tile + u)

    exchange_table[...] = table[...].astype(jnp.bfloat16)
    ice_copies[0].wait()
    border(0)

    def first_units(u, _):
        widen(0, u)
        return 0

    lax.fori_loop(0, bands * NFSD, first_units, 0, unroll=2)
    weight_copy.wait()
    for w in range(9):
        scaled[w] = weight_buf[w].astype(jnp.float32) * np.float32(1.0 / 4096.0)
    stencil(0, 0, 0)
    for n in range(NCAT):
        if n + 1 < NCAT:
            ice_copies[n + 1].wait()
            if n + 2 < NCAT:
                ice_copies[n + 2].start()
            border(n + 1)

            def both(h, _):
                pair(n, h * 2, False)
                return 0

            lax.fori_loop(0, tiles // 2 - 1, both, 0)
            pair(n, tiles - 2, True)
            out_copies[n].start()
        else:

            def band_copy(i):
                rows = pl.ds(pl.multiple_of(i * SUB, SUB), SUB)
                return pltpu.make_async_copy(
                    out_buf.at[category(n), rows, :], out.at[category(n), rows, :],
                    out_sem.at[n + i],
                )

            def one_band(i, _):
                for h in range(per_band // 2):
                    pair(n, i * per_band + h * 2, False)
                band_copy(i).start()
                return 0

            lax.fori_loop(0, bands - 1, one_band, 0)
            for h in range(per_band // 2 - 1):
                pair(n, tiles - per_band + h * 2, False)
            pair(n, tiles - 2, True)
            band_copy(bands - 1).start()
            for i in range(bands):
                band_copy(i).wait()
    for copy in out_copies:
        copy.wait()


def advance(
    cover, ice, weld, received, rows_a, rows_b, west_col, east_col, weights,
    blk_count, lat_count, cells,
):
    planes, tile_rows, tile_cols = ice.shape
    chunks = tile_cols // LANES
    bands = tile_rows // SUB
    table = jnp.asarray(weld_table().astype(np.float32))
    hbm = pl.BlockSpec(memory_space=pl.ANY)
    small = [cover, weld, received, rows_a, rows_b, west_col, east_col, table]
    held = [pltpu.with_memory_space_constraint(array, pltpu.HBM) for array in [ice, weights] + small]
    tile = pltpu.VMEM((tile_rows, tile_cols), jnp.float32)
    ext = pltpu.VMEM((3, NFSD * (chunks * EXT + 1), LANES), jnp.float32)
    moved = pltpu.VMEM((NFSD * SUB, 2 * LANES), jnp.float32)
    stacked = pltpu.VMEM((2 * LANES, 2 * LANES), jnp.bfloat16)
    return pl.pallas_call(
        functools.partial(step_kernel, blk_count, lat_count, cells),
        out_shape=jax.ShapeDtypeStruct(ice.shape, jnp.float32),
        in_specs=[hbm] * 10,
        out_specs=hbm,
        scratch_shapes=[
            pltpu.SMEM(cover.shape, jnp.int32),
            *[pltpu.VMEM(array.shape, jnp.float32) for array in small[1:]],
            pltpu.VMEM(ice.shape, jnp.float32),
            pltpu.VMEM(ice.shape, jnp.float32),
            pltpu.VMEM(weights.shape, jnp.int32),
            ext, ext,
            pltpu.VMEM(weights.shape, jnp.float32),
            tile, tile,
            pltpu.VMEM((2, 3, chunks, 64, LANES), jnp.float32),
            pltpu.VMEM((2, tile_rows, LANES), jnp.float32),
            moved, moved, stacked, stacked,
            pltpu.VMEM((NFSD * SUB, 2 * LANES), jnp.bfloat16),
            pltpu.SemaphoreType.DMA((len(small),)),
            pltpu.SemaphoreType.DMA((NCAT,)),
            pltpu.SemaphoreType.DMA,
            pltpu.SemaphoreType.DMA((NCAT - 1 + bands,)),
        ],
        compiler_params=pltpu.CompilerParams(vmem_limit_bytes=VMEM_LIMIT),
        name="advance",
    )(*held)


def on_device(ice_area, departure_weights, weld_rate, ice_cover, wave_ocean, ocean_route):
    cat_count, floe_count, tile_rows, tile_cols = ice_area.shape
    lat_count = lax.axis_size("lat")
    blk_count = lax.axis_size("blk")
    assert lat_count % 2 == 0 and blk_count % 2 == 0 and blk_count > 2
    cells = wave_ocean.shape[3]
    ice = ice_area.reshape(cat_count * floe_count, tile_rows, tile_cols)
    message, rows_a, rows_b = pack_wave(ice, wave_ocean[0], ocean_route, blk_count, lat_count)
    to_west, to_east = pack_halo(ice, message)
    received = lax.all_to_all(message, AXES, split_axis=0, concat_axis=0, tiled=True)

    pairs_a, pairs_b = [], []
    for b in range(blk_count):
        for l in range(lat_count):
            here = b * lat_count + l
            pairs_a.append((here, here ^ 1))
            if l == lat_count - 1:
                pairs_b.append((here, (blk_count - 1 - b) * lat_count + l))
            elif l > 0:
                pairs_b.append((here, here + 1 if l % 2 else here - 1))
    from_a = lax.ppermute(rows_a, AXES, pairs_a)
    from_b = lax.ppermute(rows_b, AXES, pairs_b)
    ring = [(b, (b + 1) % blk_count) for b in range(blk_count)]
    west_col = lax.ppermute(to_east, "blk", ring)
    east_col = lax.ppermute(to_west, "blk", [(b, a) for a, b in ring])
    result = advance(
        ice_cover.reshape(1, tile_rows), ice, weld_rate, received, from_a, from_b,
        west_col, east_col, departure_weights, blk_count, lat_count, cells,
    )
    return result.reshape(ice_area.shape)


def solution(mesh):
    return jax.shard_map(
        on_device,
        mesh=mesh,
        in_specs=(
            P(None, None, "lat", "blk"),
            P(None, "lat", "blk"),
            P("lat", "blk"),
            P("lat", "blk"),
            P(("blk", "lat"), None, None, None),
            P(("blk", "lat"), None),
        ),
        out_specs=P(None, None, "lat", "blk"),
        check_vma=False,
    )
```

```python
import functools

import jax
import jax.numpy as jnp
import ml_dtypes
import numpy as np
from jax import lax
from jax.experimental import pallas as pl
from jax.experimental.pallas import tpu as pltpu
from jax.sharding import PartitionSpec as P

NCAT = 5
NFSD = 12
FREQ = 25
PLANES = NCAT * NFSD
LANES = 128
SUB = 8
EXT = 41
VMEM_LIMIT = 56 * 1024 * 1024
AXES = ("blk", "lat")

fracture_step = 0.1
weld_scale = 840.0 / 1024.0


def weld_table():
    index = np.arange(NFSD)
    apart = index[:, None] - index[None, :]
    exact = np.where(apart > 0, 1.0, -1.0) / (1.0 + np.abs(apart)) * weld_scale
    high = exact.astype(ml_dtypes.bfloat16).astype(np.float64)
    low = exact - high
    kept = [0, 1, 2, 3, 8, 9, 10, 11]
    assert not np.delete(low, kept, axis=1).any()
    joined = np.concatenate([high, high, low[:, kept]], axis=1)
    return np.kron(joined, np.eye(SUB)).astype(ml_dtypes.bfloat16)


def turn_table():
    right = np.roll(np.eye(LANES), 1, axis=1)
    return np.tile(np.concatenate([right, right.T], axis=1), (2, 1)).astype(np.float32)


def turned(whole, table):
    high = whole.astype(jnp.bfloat16)
    low = (whole - high.astype(jnp.float32)).astype(jnp.bfloat16)
    both = jnp.dot(
        jnp.concatenate([high, low], axis=1), table, preferred_element_type=jnp.float32
    )
    return both[:, :LANES], both[:, LANES:]


def gather_edges(west_buf, east_buf, copies, planes, bands_of):
    lane = lax.broadcasted_iota(jnp.int32, (SUB, LANES), 1)
    west = [jnp.zeros((SUB, LANES), jnp.float32) for _ in bands_of]
    east = list(west)
    for p in range(planes):
        if p % NFSD == 0:
            for copy in copies[p // NFSD]:
                copy.wait()
        for i, start in enumerate(bands_of):
            band = slice(start, start + SUB)
            ends = jnp.where(lane == 0, west_buf[p, band, :], east_buf[p, band, :])
            ends = pltpu.roll(ends, p, 1) if p else ends
            west[i] = jnp.where(lane == p, ends, west[i])
            east[i] = jnp.where(lane == (p - 1) % LANES, ends, east[i])
    return west, [pltpu.roll(part, 1, 1) for part in east]


def wave_kernel(
    blk_count, lat_count, wave, ice, route_hbm, message, rows_a, rows_b,
    edge_rows, route, wave_buf, west_buf, east_buf, sums, corners, route_sem, wave_sem, col_sem, row_sem, send_sem,
):
    freq_count, dests, cells = wave.shape
    planes, tile_rows, tile_cols = ice.shape
    me_b = lax.axis_index("blk")
    me_l = lax.axis_index("lat")

    odd = lax.rem(me_l, 2) == 1
    first = jnp.where(odd, 0, tile_rows - 1)
    second = jnp.where(odd, tile_rows - 1, 0)
    chunks = tile_cols // LANES
    row_copies = []
    for j in range(chunks):
        for which, row in enumerate((first, second)):
            row_copies.append(
                pltpu.make_async_copy(
                    ice.at[:, row, pl.ds(j * LANES, LANES)],
                    edge_rows.at[which, j, pl.ds(0, planes), :],
                    row_sem.at[which, j],
                )
            )
    send_copies = [
        pltpu.make_async_copy(edge_rows.at[which], out, send_sem.at[which])
        for which, out in enumerate((rows_a, rows_b))
    ]
    for copy in row_copies:
        copy.start()
    col_copies = []
    for p in range(NCAT):
        own = pl.ds(p * NFSD, NFSD)
        col_copies.append(
            [
                pltpu.make_async_copy(
                    ice.at[own, pl.ds(row, SUB), pl.ds(start, LANES)],
                    buf.at[own, pl.ds(e * SUB, SUB), :],
                    col_sem.at[p, side, e],
                )
                for side, (buf, start) in enumerate(
                    ((west_buf, 0), (east_buf, tile_cols - LANES))
                )
                for e, row in enumerate((0, tile_rows - SUB))
            ]
        )
    groups = wave_sem.shape[0]
    step = dests // groups
    wave_copies = []
    for p in range(groups):
        own = pl.ds(p * step, step)
        wave_copies.append(
            pltpu.make_async_copy(wave.at[:, own, :], wave_buf.at[:, own, :], wave_sem.at[p])
        )
    route_copy = pltpu.make_async_copy(route_hbm, route, route_sem)
    route_copy.start()
    for copies in col_copies + [wave_copies]:
        for copy in copies:
            copy.start()

    ends = gather_edges(west_buf, east_buf, col_copies, planes, (0, SUB))
    for copy in row_copies:
        copy.wait()
    for copy in send_copies:
        copy.start()
    for side in range(2):
        corners[2 * side : 2 * side + 1, :] = ends[side][0][0:1, :]
        corners[2 * side + 1 : 2 * side + 2, :] = ends[side][1][SUB - 1 : SUB, :]

    for group in range(dests // SUB):
        band = slice(SUB * group, SUB * group + SUB)
        if group * SUB % step == 0:
            wave_copies[group * SUB // step].wait()
        for j in range(cells // LANES):
            chunk = slice(LANES * j, LANES * j + LANES)
            total = wave_buf[0, band, chunk] * np.float32(1.0 / freq_count)
            for f in range(1, freq_count):
                total = total + wave_buf[f, band, chunk] * np.float32((f + 1.0) / freq_count)
            sums[j, band, :] = total

    route_copy.wait()
    side_of = []
    for to_b in range(blk_count):
        last_col = (to_b == lax.rem(me_b + 1, blk_count)) | (
            to_b == lax.rem(2 * blk_count - 2 - me_b, blk_count)
        )
        side_of.append(jnp.where(last_col, 2, 0))
    row_of = [jnp.where(to_l < me_l, 0, 1) for to_l in range(lat_count)]
    for m in range(dests):
        to = route[0, m]
        for j in range(cells // LANES):
            message[to, :, LANES * j : LANES * j + LANES] = sums[j, m : m + 1, :]
        which = side_of[m // lat_count] + row_of[m % lat_count]
        message[m, :, cells : cells + LANES] = corners[pl.ds(which, 1), :]
    for copy in send_copies:
        copy.wait()


def pack_wave(ice, wave, route, blk_count, lat_count):
    planes, tile_rows, tile_cols = ice.shape
    freq_count, dests, cells = wave.shape
    chunks = tile_cols // LANES
    hbm = pl.BlockSpec(memory_space=pl.ANY)
    return pl.pallas_call(
        functools.partial(wave_kernel, blk_count, lat_count),
        out_shape=(
            jax.ShapeDtypeStruct((dests, 1, cells + LANES), jnp.float32),
            pltpu.HBM((chunks, 64, LANES), jnp.float32),
            pltpu.HBM((chunks, 64, LANES), jnp.float32),
        ),
        in_specs=[hbm] * 3,
        out_specs=(pl.BlockSpec(memory_space=pltpu.VMEM), hbm, hbm),
        scratch_shapes=[
            pltpu.VMEM((2, chunks, 64, LANES), jnp.float32),
            pltpu.SMEM(route.shape, jnp.int32),
            pltpu.VMEM((freq_count, dests, cells), jnp.float32),
            pltpu.VMEM((planes, 2 * SUB, LANES), jnp.float32),
            pltpu.VMEM((planes, 2 * SUB, LANES), jnp.float32),
            pltpu.VMEM((cells // LANES, dests, LANES), jnp.float32),
            pltpu.VMEM((SUB, LANES), jnp.float32),
            pltpu.SemaphoreType.DMA,
            pltpu.SemaphoreType.DMA((4,)),
            pltpu.SemaphoreType.DMA((NCAT, 2, 2)),
            pltpu.SemaphoreType.DMA((2, chunks)),
            pltpu.SemaphoreType.DMA((2,)),
        ],
        compiler_params=pltpu.CompilerParams(vmem_limit_bytes=VMEM_LIMIT),
        name="pack_wave",
    )(*[pltpu.with_memory_space_constraint(array, pltpu.HBM) for array in (wave, ice, route)])


def halo_kernel(ice, after, to_west, to_east, west_buf, east_buf, col_sem):
    planes, tile_rows, tile_cols = ice.shape
    bands = tile_rows // SUB
    col_copies = []
    for p in range(NCAT):
        own = pl.ds(p * NFSD, NFSD)
        col_copies.append(
            [
                pltpu.make_async_copy(
                    ice.at[own, :, pl.ds(start, LANES)], buf.at[own], col_sem.at[p, side]
                )
                for side, (buf, start) in enumerate(
                    ((west_buf, 0), (east_buf, tile_cols - LANES))
                )
            ]
        )
    for copies in col_copies:
        for copy in copies:
            copy.start()

    lane = lax.broadcasted_iota(jnp.int32, (SUB, LANES), 1)
    ends = gather_edges(
        west_buf, east_buf, col_copies, planes, tuple(range(0, tile_rows, SUB))
    )
    for parts_of, out in zip(ends, (to_west, to_east)):
        for i in range(bands // 2):
            out[SUB * i : SUB * i + SUB, :] = jnp.where(
                lane < 64, parts_of[i], pltpu.roll(parts_of[bands // 2 + i], 64, 1)
            )


def pack_halo(ice, after):
    planes, tile_rows, tile_cols = ice.shape
    hbm = pl.BlockSpec(memory_space=pl.ANY)
    vmem = pl.BlockSpec(memory_space=pltpu.VMEM)
    column = pltpu.VMEM((tile_rows // 2, LANES), jnp.float32)
    return pl.pallas_call(
        halo_kernel,
        out_shape=(column, column),
        in_specs=[hbm, hbm],
        out_specs=(vmem,) * 2,
        scratch_shapes=[
            pltpu.VMEM((planes, tile_rows, LANES), jnp.float32),
            pltpu.VMEM((planes, tile_rows, LANES), jnp.float32),
            pltpu.SemaphoreType.DMA((NCAT, 2)),
        ],
        compiler_params=pltpu.CompilerParams(vmem_limit_bytes=VMEM_LIMIT),
        name="pack_halo",
    )(*[pltpu.with_memory_space_constraint(array, pltpu.HBM) for array in (ice, after)])


def shifted(pieces, west, east):
    lane = lax.broadcasted_iota(jnp.int32, (SUB, LANES), 1)
    chunks = len(pieces)
    to_right = [pltpu.roll(piece, 1, 1) for piece in pieces]
    to_left = [pltpu.roll(piece, LANES - 1, 1) for piece in pieces]
    from_west = [to_right[0] if west is None else jnp.where(lane == 0, west, to_right[0])] + [
        jnp.where(lane == 0, to_right[j - 1], to_right[j]) for j in range(1, chunks)
    ]
    from_east = [
        jnp.where(lane == LANES - 1, to_left[j + 1], to_left[j]) for j in range(chunks - 1)
    ]
    from_east.append(
        to_left[-1] if east is None else jnp.where(lane == LANES - 1, east, to_left[-1])
    )
    return from_west, pieces, from_east


def step_kernel(
    blk_count, lat_count, cells,
    ice, weights, cover_hbm, weld_hbm, received_hbm, rows_a_hbm, rows_b_hbm, west_hbm, east_hbm,
    table_hbm, turning_hbm, out,
    cover, weld, received, rows_a, rows_b, west_col, east_col, table, turning,
    ice_buf, out_buf, weight_buf, ext_even, ext_odd, scaled, weld_now, rate, ghosts, cols,
    moved_even, moved_odd, stacked_even, stacked_odd, exchange_table,
    lane_table, corner_lanes, small_sem, ice_sem, weight_sem, out_sem,
):
    tile_rows, tile_cols = weld.shape
    bands = tile_rows // SUB
    chunks = tile_cols // LANES
    plane_pitch = chunks * EXT + 1
    lane = lax.broadcasted_iota(jnp.int32, (SUB, LANES), 1)
    sublane = lax.broadcasted_iota(jnp.int32, (SUB, LANES), 0)
    me_b = lax.axis_index("blk")
    me_l = lax.axis_index("lat")
    exts = (ext_even, ext_odd)
    moveds = (moved_even, moved_odd)
    stackeds = (stacked_even, stacked_odd)

    def category(n):
        return pl.ds(n * NFSD, NFSD)

    small_copies = [
        pltpu.make_async_copy(source, to, small_sem.at[c])
        for c, (source, to) in enumerate(
            (
                (rows_a_hbm, rows_a), (rows_b_hbm, rows_b), (west_hbm, west_col),
                (east_hbm, east_col), (received_hbm, received), (cover_hbm, cover),
                (weld_hbm, weld), (table_hbm, table), (turning_hbm, turning),
            )
        )
    ]
    ice_copies = [
        pltpu.make_async_copy(ice.at[category(n)], ice_buf.at[category(n)], ice_sem.at[n])
        for n in range(NCAT)
    ]
    weight_copy = pltpu.make_async_copy(weights, weight_buf, weight_sem)
    out_copies = [
        pltpu.make_async_copy(out_buf.at[category(n)], out.at[category(n)], out_sem.at[n])
        for n in range(NCAT - 1)
    ]
    for copy in small_copies:
        copy.start()
    ice_copies[0].start()
    weight_copy.start()
    ice_copies[1].start()
    for copy in small_copies:
        copy.wait()

    top = me_l == lat_count - 1
    bottom = me_l == 0
    odd = lax.rem(me_l, 2) == 1
    west_b = lax.rem(me_b + blk_count - 1, blk_count)
    east_b = lax.rem(me_b + 1, blk_count)
    above_l = jnp.minimum(me_l + 1, lat_count - 1)
    below_l = jnp.maximum(me_l - 1, 0)

    half = tile_rows // 2
    for side, column in enumerate((west_col, east_col)):
        for i in range(bands // 2):
            packed = column[SUB * i : SUB * i + SUB, :]
            cols[side, SUB * i : SUB * i + SUB, :] = packed
            cols[side, half + SUB * i : half + SUB * i + SUB, :] = pltpu.roll(packed, 64, 1)

    def corner(b, l):
        line = received[b * lat_count + l, :, cells : cells + LANES]
        spread = jnp.broadcast_to(line, (SUB, LANES))
        return [
            jnp.sum(jnp.where(lane == SUB * q + sublane, spread, 0.0), axis=1, keepdims=True)
            for q in range(SUB)
        ]

    below_corners = [corner(b, below_l) for b in (west_b, east_b)]
    above_corners = [
        corner(jnp.where(top, fold_b, b), above_l)
        for fold_b, b in (
            (lax.rem(blk_count - me_b, blk_count), west_b),
            (lax.rem(2 * blk_count - 2 - me_b, blk_count), east_b),
        )
    ]
    backwards = LANES - 1 - lane

    def both_sides(q, _):
        band = pl.ds(pl.multiple_of(SUB * q, SUB), SUB)
        below = [
            jnp.where(bottom, 0.0, jnp.where(odd, rows_a[j, band, :], rows_b[j, band, :]))
            for j in range(chunks)
        ]
        above = [jnp.where(odd, rows_b[j, band, :], rows_a[j, band, :]) for j in range(chunks)]
        folded = [
            jnp.take_along_axis(above[chunks - 1 - j], backwards, axis=1) for j in range(chunks)
        ]
        above = [jnp.where(top, folded[j], above[j]) for j in range(chunks)]
        right, left = turned(jnp.concatenate(below + above, axis=0), lane_table[...])
        for side, pieces in enumerate((below, above)):
            at = [slice(SUB * c, SUB * c + SUB) for c in range(side * chunks, (side + 1) * chunks)]
            to_right = [corner_lanes[2 * side, band, :]] + [right[c] for c in at]
            to_left = [left[c] for c in at] + [corner_lanes[2 * side + 1, band, :]]
            for j in range(chunks):
                ghosts[side, 0, j, band, :] = jnp.where(lane == 0, to_right[j], to_right[j + 1])
                ghosts[side, 1, j, band, :] = pieces[j]
                ghosts[side, 2, j, band, :] = jnp.where(
                    lane == LANES - 1, to_left[j + 1], to_left[j]
                )
        return 0

    for side, corners in enumerate((below_corners, above_corners)):
        for s in range(2):
            for q in range(SUB):
                end = jnp.broadcast_to(corners[s][q], (SUB, LANES))
                if side == 0:
                    end = jnp.where(bottom, 0.0, end)
                corner_lanes[2 * side + s, SUB * q : SUB * q + SUB, :] = end
    lane_table[...] = turning[...].astype(jnp.bfloat16)
    lax.fori_loop(0, SUB, both_sides, 0, unroll=4)

    per_row = tile_cols // cells
    for r in range(tile_rows):
        for j in range(chunks):
            o = r * per_row + j * LANES // cells
            start = j * LANES % cells
            rate[r : r + 1, LANES * j : LANES * j + LANES] = received[o, :, start : start + LANES]
    for i in range(bands):
        mask = jnp.zeros((SUB, LANES), jnp.float32)
        for r in range(SUB):
            here = (cover[0, SUB * i + r] > 0).astype(jnp.float32)
            mask = jnp.where(sublane == r, here, mask)
        for j in range(chunks):
            own = (slice(SUB * i, SUB * i + SUB), slice(LANES * j, LANES * j + LANES))
            rate[own] = rate[own] * (mask * np.float32(fracture_step / 11.0))
            weld_now[own] = weld[own] * mask * np.float32(0.06 / weld_scale)

    def border(n):
        ext = exts[n % 2]
        for side in range(2):
            row = 7 if side == 0 else 8 + tile_rows
            for dx in range(3):
                for j in range(chunks):
                    for k0 in (0, NFSD - SUB):
                        start = k0 * plane_pitch + j * EXT + row
                        ext[dx, pl.ds(start, SUB, stride=plane_pitch), :] = ghosts[
                            side, dx, j, pl.ds(n * NFSD + k0, SUB), :
                        ]

    def widen(n, units):
        ext = exts[n % 2]
        pieces, places = [], []
        for unit in units:
            i = unit // NFSD
            k = unit - i * NFSD
            rows = pl.ds(pl.multiple_of(i * SUB, SUB), SUB)
            places.append((i, k, rows))
            pieces += [
                ice_buf[n * NFSD + k, rows, LANES * j : LANES * j + LANES] for j in range(chunks)
            ]
        right, left = turned(jnp.concatenate(pieces, axis=0), lane_table[...])
        for u, (i, k, rows) in enumerate(places):
            p = n * NFSD + k
            at = [slice(SUB * c, SUB * c + SUB) for c in range(u * chunks, (u + 1) * chunks)]
            to_right = [pltpu.roll(cols[0, rows, :], LANES - p, 1)] + [right[c] for c in at]
            to_left = [left[c] for c in at] + [pltpu.roll(cols[1, rows, :], LANES - 1 - p, 1)]
            base = k * plane_pitch + SUB + i * SUB
            for j in range(chunks):
                own = pl.ds(base + j * EXT, SUB)
                ext[0, own, :] = to_right[j + 1]
                pltpu.store(ext.at[0, own, :], to_right[j], mask=lane == 0)
                ext[1, own, :] = pieces[u * chunks + j]
                ext[2, own, :] = to_left[j]
                pltpu.store(ext.at[2, own, :], to_left[j + 1], mask=lane == LANES - 1)

    def widen_by_rolls(n, unit):
        ext = exts[n % 2]
        i = unit // NFSD
        k = unit - i * NFSD
        p = n * NFSD + k
        rows = pl.ds(pl.multiple_of(i * SUB, SUB), SUB)
        pieces = [ice_buf[p, rows, LANES * j : LANES * j + LANES] for j in range(chunks)]
        west = pltpu.roll(cols[0, rows, :], LANES - p, 1)
        east = pltpu.roll(cols[1, rows, :], LANES - 1 - p, 1)
        to_right = [west] + [pltpu.roll(piece, 1, 1) for piece in pieces]
        to_left = [pltpu.roll(piece, LANES - 1, 1) for piece in pieces] + [east]
        base = k * plane_pitch + SUB + i * SUB
        for j in range(chunks):
            own = pl.ds(base + j * EXT, SUB)
            ext[0, own, :] = to_right[j + 1]
            pltpu.store(ext.at[0, own, :], to_right[j], mask=lane == 0)
            ext[1, own, :] = pieces[j]
            ext[2, own, :] = to_left[j]
            pltpu.store(ext.at[2, own, :], to_left[j + 1], mask=lane == LANES - 1)

    width = moved_even.shape[1] // LANES
    span = LANES * width
    per_band = chunks // width
    tiles = bands * per_band

    def place(t):
        return t // per_band, lax.rem(t, per_band)

    def stencil(n, t, slot):
        ext, moved, stacked = exts[n % 2], moveds[slot], stackeds[slot]
        i, jj = place(t)
        rows = pl.ds(pl.multiple_of(i * SUB, SUB), SUB)
        for s in range(width):
            j = jj * width + s
            columns = pl.ds(pl.multiple_of(j * LANES, LANES), LANES)
            factors = [scaled[w, rows, columns] for w in range(9)]
            base = j * EXT + i * SUB + 7
            for k in range(NFSD):
                total = None
                for w in range(9):
                    dy, dx = w // 3, w % 3
                    term = factors[w] * ext[dx, pl.ds(base + k * plane_pitch + dy, SUB), :]
                    total = term if total is None else total + term
                moved[SUB * k : SUB * k + SUB, LANES * s : LANES * s + LANES] = total
        whole = moved[...]
        high = whole.astype(jnp.bfloat16)
        low = (whole - high.astype(jnp.float32)).astype(jnp.bfloat16)
        stacked[...] = jnp.concatenate([high, low, high[: 4 * SUB], high[8 * SUB :]], axis=0)

    def exchange_of(slot):
        return jnp.dot(exchange_table[...], stackeds[slot][...], preferred_element_type=jnp.float32)

    def finish(n, t, slot, exchange):
        moved = moveds[slot]
        i, jj = place(t)
        rows = pl.ds(pl.multiple_of(i * SUB, SUB), SUB)
        columns = pl.ds(pl.multiple_of(jj * span, span), span)
        share = np.float32(1.0 / (1.0 + 0.5 * n))
        for s in range(width):
            own_columns = slice(LANES * s, LANES * s + LANES)
            columns = pl.ds(pl.multiple_of(jj * span + LANES * s, LANES), LANES)
            speed = weld_now[rows, columns]
            breaking = rate[rows, columns] * share
            carried = None
            area = moved[SUB * NFSD - SUB : SUB * NFSD, own_columns]
            square = area * (area * np.float32(weld_scale))
            for k in range(NFSD - 1, -1, -1):
                turn = area * exchange[SUB * k : SUB * k + SUB, own_columns]
                if k == NFSD - 1:
                    turn = turn + square
                if k:
                    below = moved[SUB * k - SUB : SUB * k, own_columns]
                    square = below * (below * np.float32(weld_scale))
                    turn = turn + square
                welded = area + speed * turn
                change = carried
                if k:
                    broken = breaking * welded
                    change = broken * np.float32(-k)
                    if carried is not None:
                        change = carried + change
                    carried = broken if carried is None else carried + broken
                    area = below
                out_buf[n * NFSD + k, rows, columns] = welded + change

    per_tile = bands * NFSD // tiles

    def ahead(n, t):
        for u in range(per_tile):
            widen_by_rolls(n, t * per_tile + u)

    def pair(n, t, last):
        more = n + 1 < NCAT
        for s in range(2):
            exchange = exchange_of(s)
            if last and s == 1:
                if more:
                    ahead(n + 1, t + s)
                    stencil(n + 1, 0, 0)
                finish(n, t + s, s, exchange)
            else:
                stencil(n, t + s + 1, 1 - s)
                finish(n, t + s, s, exchange)
                if more:
                    ahead(n + 1, t + s)

    exchange_table[...] = table[...].astype(jnp.bfloat16)
    ice_copies[0].wait()
    border(0)

    def first_units(u, _):
        for half in range(2):
            widen(0, [u * NFSD + half * (NFSD // 2) + v for v in range(NFSD // 2)])
        return 0

    lax.fori_loop(0, bands, first_units, 0)
    weight_copy.wait()
    for w in range(9):
        scaled[w] = weight_buf[w].astype(jnp.float32) * np.float32(1.0 / 4096.0)
    stencil(0, 0, 0)
    for n in range(NCAT):
        if n + 1 < NCAT:
            ice_copies[n + 1].wait()
            if n + 2 < NCAT:
                ice_copies[n + 2].start()
            border(n + 1)

            def both(h, _):
                pair(n, h * 2, False)
                return 0

            lax.fori_loop(0, tiles // 2 - 1, both, 0)
            pair(n, tiles - 2, True)
            out_copies[n].start()
        else:

            def band_copy(i):
                rows = pl.ds(pl.multiple_of(i * SUB, SUB), SUB)
                return pltpu.make_async_copy(
                    out_buf.at[category(n), rows, :], out.at[category(n), rows, :],
                    out_sem.at[n + i],
                )

            def one_band(i, _):
                for h in range(per_band // 2):
                    pair(n, i * per_band + h * 2, False)
                band_copy(i).start()
                return 0

            lax.fori_loop(0, bands - 1, one_band, 0)
            for h in range(per_band // 2 - 1):
                pair(n, tiles - per_band + h * 2, False)
            pair(n, tiles - 2, True)
            band_copy(bands - 1).start()
            for i in range(bands):
                band_copy(i).wait()
    for copy in out_copies:
        copy.wait()


def advance(
    cover, ice, weld, received, rows_a, rows_b, west_col, east_col, weights,
    blk_count, lat_count, cells,
):
    planes, tile_rows, tile_cols = ice.shape
    chunks = tile_cols // LANES
    bands = tile_rows // SUB
    table = jnp.asarray(weld_table().astype(np.float32))
    turning = jnp.asarray(turn_table())
    hbm = pl.BlockSpec(memory_space=pl.ANY)
    small = [cover, weld, received, rows_a, rows_b, west_col, east_col, table, turning]
    held = [pltpu.with_memory_space_constraint(array, pltpu.HBM) for array in [ice, weights] + small]
    tile = pltpu.VMEM((tile_rows, tile_cols), jnp.float32)
    ext = pltpu.VMEM((3, NFSD * (chunks * EXT + 1), LANES), jnp.float32)
    moved = pltpu.VMEM((NFSD * SUB, 2 * LANES), jnp.float32)
    stacked = pltpu.VMEM((table.shape[1], 2 * LANES), jnp.bfloat16)
    return pl.pallas_call(
        functools.partial(step_kernel, blk_count, lat_count, cells),
        out_shape=jax.ShapeDtypeStruct(ice.shape, jnp.float32),
        in_specs=[hbm] * len(held),
        out_specs=hbm,
        scratch_shapes=[
            pltpu.SMEM(cover.shape, jnp.int32),
            *[pltpu.VMEM(array.shape, jnp.float32) for array in small[1:]],
            pltpu.VMEM(ice.shape, jnp.float32),
            pltpu.VMEM(ice.shape, jnp.float32),
            pltpu.VMEM(weights.shape, jnp.int32),
            ext, ext,
            pltpu.VMEM(weights.shape, jnp.float32),
            tile, tile,
            pltpu.VMEM((2, 3, chunks, 64, LANES), jnp.float32),
            pltpu.VMEM((2, tile_rows, LANES), jnp.float32),
            moved, moved, stacked, stacked,
            pltpu.VMEM((NFSD * SUB, 2 * LANES), jnp.bfloat16),
            pltpu.VMEM(turning.shape, jnp.bfloat16),
            pltpu.VMEM((4, 64, LANES), jnp.float32),
            pltpu.SemaphoreType.DMA((len(small),)),
            pltpu.SemaphoreType.DMA((NCAT,)),
            pltpu.SemaphoreType.DMA,
            pltpu.SemaphoreType.DMA((NCAT - 1 + bands,)),
        ],
        compiler_params=pltpu.CompilerParams(vmem_limit_bytes=VMEM_LIMIT),
        name="advance",
    )(*held)


def on_device(ice_area, departure_weights, weld_rate, ice_cover, wave_ocean, ocean_route):
    cat_count, floe_count, tile_rows, tile_cols = ice_area.shape
    lat_count = lax.axis_size("lat")
    blk_count = lax.axis_size("blk")
    assert lat_count % 2 == 0 and blk_count % 2 == 0 and blk_count > 2
    cells = wave_ocean.shape[3]
    ice = ice_area.reshape(cat_count * floe_count, tile_rows, tile_cols)
    message, rows_a, rows_b = pack_wave(ice, wave_ocean[0], ocean_route, blk_count, lat_count)
    to_west, to_east = pack_halo(ice, message)
    received = lax.all_to_all(message, AXES, split_axis=0, concat_axis=0, tiled=True)

    pairs_a, pairs_b = [], []
    for b in range(blk_count):
        for l in range(lat_count):
            here = b * lat_count + l
            pairs_a.append((here, here ^ 1))
            if l == lat_count - 1:
                pairs_b.append((here, (blk_count - 1 - b) * lat_count + l))
            elif l > 0:
                pairs_b.append((here, here + 1 if l % 2 else here - 1))
    from_a = lax.ppermute(rows_a, AXES, pairs_a)
    from_b = lax.ppermute(rows_b, AXES, pairs_b)
    ring = [(b, (b + 1) % blk_count) for b in range(blk_count)]
    west_col = lax.ppermute(to_east, "blk", ring)
    east_col = lax.ppermute(to_west, "blk", [(b, a) for a, b in ring])
    result = advance(
        ice_cover.reshape(1, tile_rows), ice, weld_rate, received, from_a, from_b,
        west_col, east_col, departure_weights, blk_count, lat_count, cells,
    )
    return result.reshape(ice_area.shape)


def solution(mesh):
    return jax.shard_map(
        on_device,
        mesh=mesh,
        in_specs=(
            P(None, None, "lat", "blk"),
            P(None, "lat", "blk"),
            P("lat", "blk"),
            P("lat", "blk"),
            P(("blk", "lat"), None, None, None),
            P(("blk", "lat"), None),
        ),
        out_specs=P(None, None, "lat", "blk"),
        check_vma=False,
    )
```

```python
import functools

import jax
import jax.numpy as jnp
import ml_dtypes
import numpy as np
from jax import lax
from jax.experimental import pallas as pl
from jax.experimental.pallas import tpu as pltpu
from jax.sharding import PartitionSpec as P

NCAT = 5
NFSD = 12
FREQ = 25
PLANES = NCAT * NFSD
LANES = 128
SUB = 8
EXT = 41
VMEM_LIMIT = 56 * 1024 * 1024
AXES = ("blk", "lat")

fracture_step = 0.1
weld_scale = 840.0 / 1024.0


def weld_table():
    index = np.arange(NFSD)
    apart = index[:, None] - index[None, :]
    exact = np.where(apart > 0, 1.0, -1.0) / (1.0 + np.abs(apart)) * weld_scale
    high = exact.astype(ml_dtypes.bfloat16).astype(np.float64)
    low = exact - high
    kept = [0, 1, 2, 3, 8, 9, 10, 11]
    assert not np.delete(low, kept, axis=1).any()
    joined = np.concatenate([high, high, low[:, kept]], axis=1)
    return np.kron(joined, np.eye(SUB)).astype(ml_dtypes.bfloat16)


def turn_table():
    right = np.roll(np.eye(LANES), 1, axis=1)
    return np.tile(np.concatenate([right, right.T], axis=1), (2, 1)).astype(np.float32)


def turned(whole, table):
    high = whole.astype(jnp.bfloat16)
    low = (whole - high.astype(jnp.float32)).astype(jnp.bfloat16)
    both = jnp.dot(
        jnp.concatenate([high, low], axis=1), table, preferred_element_type=jnp.float32
    )
    return both[:, :LANES], both[:, LANES:]


def gather_edges(west_buf, east_buf, copies, planes, bands_of):
    lane = lax.broadcasted_iota(jnp.int32, (SUB, LANES), 1)
    west = [jnp.zeros((SUB, LANES), jnp.float32) for _ in bands_of]
    east = list(west)
    for p in range(planes):
        if p % NFSD == 0:
            for copy in copies[p // NFSD]:
                copy.wait()
        for i, start in enumerate(bands_of):
            band = slice(start, start + SUB)
            ends = jnp.where(lane == 0, west_buf[p, band, :], east_buf[p, band, :])
            ends = pltpu.roll(ends, p, 1) if p else ends
            west[i] = jnp.where(lane == p, ends, west[i])
            east[i] = jnp.where(lane == (p - 1) % LANES, ends, east[i])
    return west, [pltpu.roll(part, 1, 1) for part in east]


def wave_kernel(
    blk_count, lat_count, wave, ice, route_hbm, message, rows_a, rows_b,
    edge_rows, route, wave_buf, west_buf, east_buf, sums, corners, route_sem, wave_sem, col_sem, row_sem, send_sem,
):
    freq_count, dests, cells = wave.shape
    planes, tile_rows, tile_cols = ice.shape
    me_b = lax.axis_index("blk")
    me_l = lax.axis_index("lat")

    odd = lax.rem(me_l, 2) == 1
    first = jnp.where(odd, 0, tile_rows - 1)
    second = jnp.where(odd, tile_rows - 1, 0)
    chunks = tile_cols // LANES
    row_copies = []
    for j in range(chunks):
        for which, row in enumerate((first, second)):
            row_copies.append(
                pltpu.make_async_copy(
                    ice.at[:, row, pl.ds(j * LANES, LANES)],
                    edge_rows.at[which, j, pl.ds(0, planes), :],
                    row_sem.at[which, j],
                )
            )
    send_copies = [
        pltpu.make_async_copy(edge_rows.at[which], out, send_sem.at[which])
        for which, out in enumerate((rows_a, rows_b))
    ]
    col_copies = []
    for p in range(NCAT):
        own = pl.ds(p * NFSD, NFSD)
        col_copies.append(
            [
                pltpu.make_async_copy(
                    ice.at[own, pl.ds(row, SUB), pl.ds(start, LANES)],
                    buf.at[own, pl.ds(e * SUB, SUB), :],
                    col_sem.at[p, side, e],
                )
                for side, (buf, start) in enumerate(
                    ((west_buf, 0), (east_buf, tile_cols - LANES))
                )
                for e, row in enumerate((0, tile_rows - SUB))
            ]
        )
    groups = wave_sem.shape[0]
    step = dests // groups
    wave_copies = []
    for p in range(groups):
        own = pl.ds(p * step, step)
        wave_copies.append(
            pltpu.make_async_copy(wave.at[:, own, :], wave_buf.at[:, own, :], wave_sem.at[p])
        )
    route_copy = pltpu.make_async_copy(route_hbm, route, route_sem)
    route_copy.start()
    for copies in col_copies + [wave_copies, row_copies]:
        for copy in copies:
            copy.start()

    ends = gather_edges(west_buf, east_buf, col_copies, planes, (0, SUB))
    for side in range(2):
        corners[2 * side : 2 * side + 1, :] = ends[side][0][0:1, :]
        corners[2 * side + 1 : 2 * side + 2, :] = ends[side][1][SUB - 1 : SUB, :]

    for group in range(dests // SUB):
        band = slice(SUB * group, SUB * group + SUB)
        if group * SUB % step == 0:
            wave_copies[group * SUB // step].wait()
        for j in range(cells // LANES):
            chunk = slice(LANES * j, LANES * j + LANES)
            total = wave_buf[0, band, chunk] * np.float32(1.0 / freq_count)
            for f in range(1, freq_count):
                total = total + wave_buf[f, band, chunk] * np.float32((f + 1.0) / freq_count)
            sums[j, band, :] = total

    for copy in row_copies:
        copy.wait()
    for copy in send_copies:
        copy.start()
    route_copy.wait()
    side_of = []
    for to_b in range(blk_count):
        last_col = (to_b == lax.rem(me_b + 1, blk_count)) | (
            to_b == lax.rem(2 * blk_count - 2 - me_b, blk_count)
        )
        side_of.append(jnp.where(last_col, 2, 0))
    row_of = [jnp.where(to_l < me_l, 0, 1) for to_l in range(lat_count)]
    for m in range(dests):
        to = route[0, m]
        for j in range(cells // LANES):
            message[to, :, LANES * j : LANES * j + LANES] = sums[j, m : m + 1, :]
        which = side_of[m // lat_count] + row_of[m % lat_count]
        message[m, :, cells : cells + LANES] = corners[pl.ds(which, 1), :]
    for copy in send_copies:
        copy.wait()


def pack_wave(ice, wave, route, blk_count, lat_count):
    planes, tile_rows, tile_cols = ice.shape
    freq_count, dests, cells = wave.shape
    chunks = tile_cols // LANES
    hbm = pl.BlockSpec(memory_space=pl.ANY)
    return pl.pallas_call(
        functools.partial(wave_kernel, blk_count, lat_count),
        out_shape=(
            jax.ShapeDtypeStruct((dests, 1, cells + LANES), jnp.float32),
            pltpu.HBM((chunks, 64, LANES), jnp.float32),
            pltpu.HBM((chunks, 64, LANES), jnp.float32),
        ),
        in_specs=[hbm] * 3,
        out_specs=(pl.BlockSpec(memory_space=pltpu.VMEM), hbm, hbm),
        scratch_shapes=[
            pltpu.VMEM((2, chunks, 64, LANES), jnp.float32),
            pltpu.SMEM(route.shape, jnp.int32),
            pltpu.VMEM((freq_count, dests, cells), jnp.float32),
            pltpu.VMEM((planes, 2 * SUB, LANES), jnp.float32),
            pltpu.VMEM((planes, 2 * SUB, LANES), jnp.float32),
            pltpu.VMEM((cells // LANES, dests, LANES), jnp.float32),
            pltpu.VMEM((SUB, LANES), jnp.float32),
            pltpu.SemaphoreType.DMA,
            pltpu.SemaphoreType.DMA((4,)),
            pltpu.SemaphoreType.DMA((NCAT, 2, 2)),
            pltpu.SemaphoreType.DMA((2, chunks)),
            pltpu.SemaphoreType.DMA((2,)),
        ],
        compiler_params=pltpu.CompilerParams(vmem_limit_bytes=VMEM_LIMIT),
        name="pack_wave",
    )(*[pltpu.with_memory_space_constraint(array, pltpu.HBM) for array in (wave, ice, route)])


def halo_kernel(ice, after, to_west, to_east, west_buf, east_buf, col_sem):
    planes, tile_rows, tile_cols = ice.shape
    bands = tile_rows // SUB
    col_copies = []
    for p in range(NCAT):
        own = pl.ds(p * NFSD, NFSD)
        col_copies.append(
            [
                pltpu.make_async_copy(
                    ice.at[own, :, pl.ds(start, LANES)], buf.at[own], col_sem.at[p, side]
                )
                for side, (buf, start) in enumerate(
                    ((west_buf, 0), (east_buf, tile_cols - LANES))
                )
            ]
        )
    for copies in col_copies:
        for copy in copies:
            copy.start()

    lane = lax.broadcasted_iota(jnp.int32, (SUB, LANES), 1)
    ends = gather_edges(
        west_buf, east_buf, col_copies, planes, tuple(range(0, tile_rows, SUB))
    )
    for parts_of, out in zip(ends, (to_west, to_east)):
        for i in range(bands // 2):
            out[SUB * i : SUB * i + SUB, :] = jnp.where(
                lane < 64, parts_of[i], pltpu.roll(parts_of[bands // 2 + i], 64, 1)
            )


def pack_halo(ice, after):
    planes, tile_rows, tile_cols = ice.shape
    hbm = pl.BlockSpec(memory_space=pl.ANY)
    vmem = pl.BlockSpec(memory_space=pltpu.VMEM)
    column = pltpu.VMEM((tile_rows // 2, LANES), jnp.float32)
    return pl.pallas_call(
        halo_kernel,
        out_shape=(column, column),
        in_specs=[hbm, hbm],
        out_specs=(vmem,) * 2,
        scratch_shapes=[
            pltpu.VMEM((planes, tile_rows, LANES), jnp.float32),
            pltpu.VMEM((planes, tile_rows, LANES), jnp.float32),
            pltpu.SemaphoreType.DMA((NCAT, 2)),
        ],
        compiler_params=pltpu.CompilerParams(vmem_limit_bytes=VMEM_LIMIT),
        name="pack_halo",
    )(*[pltpu.with_memory_space_constraint(array, pltpu.HBM) for array in (ice, after)])


def shifted(pieces, west, east):
    lane = lax.broadcasted_iota(jnp.int32, (SUB, LANES), 1)
    chunks = len(pieces)
    to_right = [pltpu.roll(piece, 1, 1) for piece in pieces]
    to_left = [pltpu.roll(piece, LANES - 1, 1) for piece in pieces]
    from_west = [to_right[0] if west is None else jnp.where(lane == 0, west, to_right[0])] + [
        jnp.where(lane == 0, to_right[j - 1], to_right[j]) for j in range(1, chunks)
    ]
    from_east = [
        jnp.where(lane == LANES - 1, to_left[j + 1], to_left[j]) for j in range(chunks - 1)
    ]
    from_east.append(
        to_left[-1] if east is None else jnp.where(lane == LANES - 1, east, to_left[-1])
    )
    return from_west, pieces, from_east


def step_kernel(
    blk_count, lat_count, cells,
    ice, weights, cover_hbm, weld_hbm, received_hbm, rows_a_hbm, rows_b_hbm, west_hbm, east_hbm,
    table_hbm, turning_hbm, out,
    cover, weld, received, rows_a, rows_b, west_col, east_col, table, turning,
    ice_buf, out_buf, weight_buf, ext_even, ext_odd, scaled, weld_now, rate, ghosts, cols,
    moved_even, moved_odd, stacked_even, stacked_odd, exchange_table,
    lane_table, corner_lanes, small_sem, ice_sem, weight_sem, out_sem,
):
    tile_rows, tile_cols = weld.shape
    bands = tile_rows // SUB
    chunks = tile_cols // LANES
    plane_pitch = chunks * EXT + 1
    lane = lax.broadcasted_iota(jnp.int32, (SUB, LANES), 1)
    sublane = lax.broadcasted_iota(jnp.int32, (SUB, LANES), 0)
    me_b = lax.axis_index("blk")
    me_l = lax.axis_index("lat")
    exts = (ext_even, ext_odd)
    moveds = (moved_even, moved_odd)
    stackeds = (stacked_even, stacked_odd)

    def category(n):
        return pl.ds(n * NFSD, NFSD)

    small_copies = [
        pltpu.make_async_copy(source, to, small_sem.at[c])
        for c, (source, to) in enumerate(
            (
                (rows_a_hbm, rows_a), (rows_b_hbm, rows_b), (west_hbm, west_col),
                (east_hbm, east_col), (received_hbm, received), (cover_hbm, cover),
                (weld_hbm, weld), (table_hbm, table), (turning_hbm, turning),
            )
        )
    ]
    ice_copies = [
        pltpu.make_async_copy(ice.at[category(n)], ice_buf.at[category(n)], ice_sem.at[n])
        for n in range(NCAT)
    ]
    weight_copy = pltpu.make_async_copy(weights, weight_buf, weight_sem)
    out_copies = [
        pltpu.make_async_copy(out_buf.at[category(n)], out.at[category(n)], out_sem.at[n])
        for n in range(NCAT - 1)
    ]
    for copy in small_copies:
        copy.start()
    ice_copies[0].start()
    weight_copy.start()
    ice_copies[1].start()
    for copy in small_copies:
        copy.wait()

    top = me_l == lat_count - 1
    bottom = me_l == 0
    odd = lax.rem(me_l, 2) == 1
    west_b = lax.rem(me_b + blk_count - 1, blk_count)
    east_b = lax.rem(me_b + 1, blk_count)
    above_l = jnp.minimum(me_l + 1, lat_count - 1)
    below_l = jnp.maximum(me_l - 1, 0)

    half = tile_rows // 2
    for side, column in enumerate((west_col, east_col)):
        for i in range(bands // 2):
            packed = column[SUB * i : SUB * i + SUB, :]
            cols[side, SUB * i : SUB * i + SUB, :] = packed
            cols[side, half + SUB * i : half + SUB * i + SUB, :] = pltpu.roll(packed, 64, 1)

    def corner(b, l):
        line = received[b * lat_count + l, :, cells : cells + LANES]
        spread = jnp.broadcast_to(line, (SUB, LANES))
        return [
            jnp.sum(jnp.where(lane == SUB * q + sublane, spread, 0.0), axis=1, keepdims=True)
            for q in range(SUB)
        ]

    below_corners = [corner(b, below_l) for b in (west_b, east_b)]
    above_corners = [
        corner(jnp.where(top, fold_b, b), above_l)
        for fold_b, b in (
            (lax.rem(blk_count - me_b, blk_count), west_b),
            (lax.rem(2 * blk_count - 2 - me_b, blk_count), east_b),
        )
    ]
    backwards = LANES - 1 - lane

    def both_sides(q, _):
        band = pl.ds(pl.multiple_of(SUB * q, SUB), SUB)
        below = [
            jnp.where(bottom, 0.0, jnp.where(odd, rows_a[j, band, :], rows_b[j, band, :]))
            for j in range(chunks)
        ]
        above = [jnp.where(odd, rows_b[j, band, :], rows_a[j, band, :]) for j in range(chunks)]
        folded = [
            jnp.take_along_axis(above[chunks - 1 - j], backwards, axis=1) for j in range(chunks)
        ]
        above = [jnp.where(top, folded[j], above[j]) for j in range(chunks)]
        right, left = turned(jnp.concatenate(below + above, axis=0), lane_table[...])
        for side, pieces in enumerate((below, above)):
            at = [slice(SUB * c, SUB * c + SUB) for c in range(side * chunks, (side + 1) * chunks)]
            to_right = [corner_lanes[2 * side, band, :]] + [right[c] for c in at]
            to_left = [left[c] for c in at] + [corner_lanes[2 * side + 1, band, :]]
            for j in range(chunks):
                ghosts[side, 0, j, band, :] = jnp.where(lane == 0, to_right[j], to_right[j + 1])
                ghosts[side, 1, j, band, :] = pieces[j]
                ghosts[side, 2, j, band, :] = jnp.where(
                    lane == LANES - 1, to_left[j + 1], to_left[j]
                )
        return 0

    for side, corners in enumerate((below_corners, above_corners)):
        for s in range(2):
            for q in range(SUB):
                end = jnp.broadcast_to(corners[s][q], (SUB, LANES))
                if side == 0:
                    end = jnp.where(bottom, 0.0, end)
                corner_lanes[2 * side + s, SUB * q : SUB * q + SUB, :] = end
    lane_table[...] = turning[...].astype(jnp.bfloat16)
    lax.fori_loop(0, SUB, both_sides, 0, unroll=4)

    per_row = tile_cols // cells
    for r in range(tile_rows):
        for j in range(chunks):
            o = r * per_row + j * LANES // cells
            start = j * LANES % cells
            rate[r : r + 1, LANES * j : LANES * j + LANES] = received[o, :, start : start + LANES]
    for i in range(bands):
        mask = jnp.zeros((SUB, LANES), jnp.float32)
        for r in range(SUB):
            here = (cover[0, SUB * i + r] > 0).astype(jnp.float32)
            mask = jnp.where(sublane == r, here, mask)
        for j in range(chunks):
            own = (slice(SUB * i, SUB * i + SUB), slice(LANES * j, LANES * j + LANES))
            rate[own] = rate[own] * (mask * np.float32(fracture_step / 11.0))
            weld_now[own] = weld[own] * mask * np.float32(0.06 / weld_scale)

    def border(n):
        ext = exts[n % 2]
        for side in range(2):
            row = 7 if side == 0 else 8 + tile_rows
            for dx in range(3):
                for j in range(chunks):
                    for k0 in (0, NFSD - SUB):
                        start = k0 * plane_pitch + j * EXT + row
                        ext[dx, pl.ds(start, SUB, stride=plane_pitch), :] = ghosts[
                            side, dx, j, pl.ds(n * NFSD + k0, SUB), :
                        ]

    def widen(n, units):
        ext = exts[n % 2]
        pieces, places = [], []
        for unit in units:
            i = unit // NFSD
            k = unit - i * NFSD
            rows = pl.ds(pl.multiple_of(i * SUB, SUB), SUB)
            places.append((i, k, rows))
            pieces += [
                ice_buf[n * NFSD + k, rows, LANES * j : LANES * j + LANES] for j in range(chunks)
            ]
        right, left = turned(jnp.concatenate(pieces, axis=0), lane_table[...])
        for u, (i, k, rows) in enumerate(places):
            p = n * NFSD + k
            at = [slice(SUB * c, SUB * c + SUB) for c in range(u * chunks, (u + 1) * chunks)]
            to_right = [pltpu.roll(cols[0, rows, :], LANES - p, 1)] + [right[c] for c in at]
            to_left = [left[c] for c in at] + [pltpu.roll(cols[1, rows, :], LANES - 1 - p, 1)]
            base = k * plane_pitch + SUB + i * SUB
            for j in range(chunks):
                own = pl.ds(base + j * EXT, SUB)
                ext[0, own, :] = to_right[j + 1]
                pltpu.store(ext.at[0, own, :], to_right[j], mask=lane == 0)
                ext[1, own, :] = pieces[u * chunks + j]
                ext[2, own, :] = to_left[j]
                pltpu.store(ext.at[2, own, :], to_left[j + 1], mask=lane == LANES - 1)

    def widen_by_rolls(n, unit):
        ext = exts[n % 2]
        i = unit // NFSD
        k = unit - i * NFSD
        p = n * NFSD + k
        rows = pl.ds(pl.multiple_of(i * SUB, SUB), SUB)
        pieces = [ice_buf[p, rows, LANES * j : LANES * j + LANES] for j in range(chunks)]
        west = pltpu.roll(cols[0, rows, :], LANES - p, 1)
        east = pltpu.roll(cols[1, rows, :], LANES - 1 - p, 1)
        to_right = [west] + [pltpu.roll(piece, 1, 1) for piece in pieces]
        to_left = [pltpu.roll(piece, LANES - 1, 1) for piece in pieces] + [east]
        base = k * plane_pitch + SUB + i * SUB
        for j in range(chunks):
            own = pl.ds(base + j * EXT, SUB)
            ext[0, own, :] = to_right[j + 1]
            pltpu.store(ext.at[0, own, :], to_right[j], mask=lane == 0)
            ext[1, own, :] = pieces[j]
            ext[2, own, :] = to_left[j]
            pltpu.store(ext.at[2, own, :], to_left[j + 1], mask=lane == LANES - 1)

    width = moved_even.shape[1] // LANES
    span = LANES * width
    per_band = chunks // width
    tiles = bands * per_band

    def place(t):
        return t // per_band, lax.rem(t, per_band)

    def stencil(n, t, slot):
        ext, moved, stacked = exts[n % 2], moveds[slot], stackeds[slot]
        i, jj = place(t)
        rows = pl.ds(pl.multiple_of(i * SUB, SUB), SUB)
        for s in range(width):
            j = jj * width + s
            columns = pl.ds(pl.multiple_of(j * LANES, LANES), LANES)
            factors = [scaled[w, rows, columns] for w in range(9)]
            base = j * EXT + i * SUB + 7
            for k in range(NFSD):
                total = None
                for w in range(9):
                    dy, dx = w // 3, w % 3
                    term = factors[w] * ext[dx, pl.ds(base + k * plane_pitch + dy, SUB), :]
                    total = term if total is None else total + term
                moved[SUB * k : SUB * k + SUB, LANES * s : LANES * s + LANES] = total
        whole = moved[...]
        high = whole.astype(jnp.bfloat16)
        low = (whole - high.astype(jnp.float32)).astype(jnp.bfloat16)
        stacked[...] = jnp.concatenate([high, low, high[: 4 * SUB], high[8 * SUB :]], axis=0)

    def exchange_of(slot):
        return jnp.dot(exchange_table[...], stackeds[slot][...], preferred_element_type=jnp.float32)

    def finish(n, t, slot, exchange):
        moved = moveds[slot]
        i, jj = place(t)
        rows = pl.ds(pl.multiple_of(i * SUB, SUB), SUB)
        columns = pl.ds(pl.multiple_of(jj * span, span), span)
        share = np.float32(1.0 / (1.0 + 0.5 * n))
        for s in range(width):
            own_columns = slice(LANES * s, LANES * s + LANES)
            columns = pl.ds(pl.multiple_of(jj * span + LANES * s, LANES), LANES)
            speed = weld_now[rows, columns]
            breaking = rate[rows, columns] * share
            carried = None
            area = moved[SUB * NFSD - SUB : SUB * NFSD, own_columns]
            square = area * (area * np.float32(weld_scale))
            for k in range(NFSD - 1, -1, -1):
                turn = area * exchange[SUB * k : SUB * k + SUB, own_columns]
                if k == NFSD - 1:
                    turn = turn + square
                if k:
                    below = moved[SUB * k - SUB : SUB * k, own_columns]
                    square = below * (below * np.float32(weld_scale))
                    turn = turn + square
                welded = area + speed * turn
                change = carried
                if k:
                    broken = breaking * welded
                    change = broken * np.float32(-k)
                    if carried is not None:
                        change = carried + change
                    carried = broken if carried is None else carried + broken
                    area = below
                out_buf[n * NFSD + k, rows, columns] = welded + change

    per_tile = bands * NFSD // tiles

    def ahead(n, t):
        for u in range(per_tile):
            widen_by_rolls(n, t * per_tile + u)

    def pair(n, t, last):
        more = n + 1 < NCAT
        for s in range(2):
            exchange = exchange_of(s)
            if last and s == 1:
                if more:
                    ahead(n + 1, t + s)
                    stencil(n + 1, 0, 0)
                finish(n, t + s, s, exchange)
            else:
                stencil(n, t + s + 1, 1 - s)
                finish(n, t + s, s, exchange)
                if more:
                    ahead(n + 1, t + s)

    exchange_table[...] = table[...].astype(jnp.bfloat16)
    ice_copies[0].wait()
    border(0)

    def first_units(u, _):
        for half in range(2):
            widen(0, [u * NFSD + half * (NFSD // 2) + v for v in range(NFSD // 2)])
        return 0

    lax.fori_loop(0, bands, first_units, 0)
    weight_copy.wait()
    for w in range(9):
        scaled[w] = weight_buf[w].astype(jnp.float32) * np.float32(1.0 / 4096.0)
    stencil(0, 0, 0)
    for n in range(NCAT):
        if n + 1 < NCAT:
            ice_copies[n + 1].wait()
            if n + 2 < NCAT:
                ice_copies[n + 2].start()
            border(n + 1)

            def both(h, _):
                pair(n, h * 2, False)
                return 0

            lax.fori_loop(0, tiles // 2 - 1, both, 0)
            pair(n, tiles - 2, True)
            out_copies[n].start()
        else:

            def band_copy(i):
                rows = pl.ds(pl.multiple_of(i * SUB, SUB), SUB)
                return pltpu.make_async_copy(
                    out_buf.at[category(n), rows, :], out.at[category(n), rows, :],
                    out_sem.at[n + i],
                )

            def one_band(i, _):
                for h in range(per_band // 2):
                    pair(n, i * per_band + h * 2, False)
                band_copy(i).start()
                return 0

            lax.fori_loop(0, bands - 1, one_band, 0)
            for h in range(per_band // 2 - 1):
                pair(n, tiles - per_band + h * 2, False)
            pair(n, tiles - 2, True)
            band_copy(bands - 1).start()
            for i in range(bands):
                band_copy(i).wait()
    for copy in out_copies:
        copy.wait()


def advance(
    cover, ice, weld, received, rows_a, rows_b, west_col, east_col, weights,
    blk_count, lat_count, cells,
):
    planes, tile_rows, tile_cols = ice.shape
    chunks = tile_cols // LANES
    bands = tile_rows // SUB
    table = jnp.asarray(weld_table().astype(np.float32))
    turning = jnp.asarray(turn_table())
    hbm = pl.BlockSpec(memory_space=pl.ANY)
    small = [cover, weld, received, rows_a, rows_b, west_col, east_col, table, turning]
    held = [pltpu.with_memory_space_constraint(array, pltpu.HBM) for array in [ice, weights] + small]
    tile = pltpu.VMEM((tile_rows, tile_cols), jnp.float32)
    ext = pltpu.VMEM((3, NFSD * (chunks * EXT + 1), LANES), jnp.float32)
    moved = pltpu.VMEM((NFSD * SUB, 2 * LANES), jnp.float32)
    stacked = pltpu.VMEM((table.shape[1], 2 * LANES), jnp.bfloat16)
    return pl.pallas_call(
        functools.partial(step_kernel, blk_count, lat_count, cells),
        out_shape=jax.ShapeDtypeStruct(ice.shape, jnp.float32),
        in_specs=[hbm] * len(held),
        out_specs=hbm,
        scratch_shapes=[
            pltpu.SMEM(cover.shape, jnp.int32),
            *[pltpu.VMEM(array.shape, jnp.float32) for array in small[1:]],
            pltpu.VMEM(ice.shape, jnp.float32),
            pltpu.VMEM(ice.shape, jnp.float32),
            pltpu.VMEM(weights.shape, jnp.int32),
            ext, ext,
            pltpu.VMEM(weights.shape, jnp.float32),
            tile, tile,
            pltpu.VMEM((2, 3, chunks, 64, LANES), jnp.float32),
            pltpu.VMEM((2, tile_rows, LANES), jnp.float32),
            moved, moved, stacked, stacked,
            pltpu.VMEM((NFSD * SUB, 2 * LANES), jnp.bfloat16),
            pltpu.VMEM(turning.shape, jnp.bfloat16),
            pltpu.VMEM((4, 64, LANES), jnp.float32),
            pltpu.SemaphoreType.DMA((len(small),)),
            pltpu.SemaphoreType.DMA((NCAT,)),
            pltpu.SemaphoreType.DMA,
            pltpu.SemaphoreType.DMA((NCAT - 1 + bands,)),
        ],
        compiler_params=pltpu.CompilerParams(vmem_limit_bytes=VMEM_LIMIT),
        name="advance",
    )(*held)


def on_device(ice_area, departure_weights, weld_rate, ice_cover, wave_ocean, ocean_route):
    cat_count, floe_count, tile_rows, tile_cols = ice_area.shape
    lat_count = lax.axis_size("lat")
    blk_count = lax.axis_size("blk")
    assert lat_count % 2 == 0 and blk_count % 2 == 0 and blk_count > 2
    cells = wave_ocean.shape[3]
    ice = ice_area.reshape(cat_count * floe_count, tile_rows, tile_cols)
    message, rows_a, rows_b = pack_wave(ice, wave_ocean[0], ocean_route, blk_count, lat_count)
    to_west, to_east = pack_halo(ice, message)
    received = lax.all_to_all(message, AXES, split_axis=0, concat_axis=0, tiled=True)

    pairs_a, pairs_b = [], []
    for b in range(blk_count):
        for l in range(lat_count):
            here = b * lat_count + l
            pairs_a.append((here, here ^ 1))
            if l == lat_count - 1:
                pairs_b.append((here, (blk_count - 1 - b) * lat_count + l))
            elif l > 0:
                pairs_b.append((here, here + 1 if l % 2 else here - 1))
    from_a = lax.ppermute(rows_a, AXES, pairs_a)
    from_b = lax.ppermute(rows_b, AXES, pairs_b)
    ring = [(b, (b + 1) % blk_count) for b in range(blk_count)]
    west_col = lax.ppermute(to_east, "blk", ring)
    east_col = lax.ppermute(to_west, "blk", [(b, a) for a, b in ring])
    result = advance(
        ice_cover.reshape(1, tile_rows), ice, weld_rate, received, from_a, from_b,
        west_col, east_col, departure_weights, blk_count, lat_count, cells,
    )
    return result.reshape(ice_area.shape)


def solution(mesh):
    return jax.shard_map(
        on_device,
        mesh=mesh,
        in_specs=(
            P(None, None, "lat", "blk"),
            P(None, "lat", "blk"),
            P("lat", "blk"),
            P("lat", "blk"),
            P(("blk", "lat"), None, None, None),
            P(("blk", "lat"), None),
        ),
        out_specs=P(None, None, "lat", "blk"),
        check_vma=False,
    )
```
